512 devices in a mesh: sub: 8 (over y), row: 64 (over z, x, core).
Axes of the slice: x: 4, y: 8, z: 8, core: 2. Of those that a mesh axis runs over, the one named last changes fastest.
Arguments:
- eigen_basis: bfloat16 [8, 48, 3, 128, 16, 128], P('sub', None, None, 'row'), may hold values from -6 to 6
- material: int32 [8, 128, 16, 128], P('sub'), may hold values from 0 to 15
- counts: int32 [8], P('sub'), may hold values from 8 to 48, as said below
- couple: int32 [8, 2], P('sub'), may hold values 0 or 1
- own_rows: int32 [8, 2, 262144], P('sub', None, 'row'), may hold values from 0 to 12287
- send_rows: int32 [8, 2, 262144], P('sub', None, 'row'), may hold values from 0 to 12287
- stiffness: float32 [16], replicated, may hold values from 0.02 to 0.2
Outputs:
- coarse_diag: float32 [8, 48, 48], P('sub')
- coarse_off: float32 [8, 4, 48, 48], P('sub')
The draws below stay inside these ranges and needn't reach their ends.
Inputs may be any that keep to these rules, and one draw needn't show every extreme that they name: Subdomain i uses its first counts[i] eigenvectors; some subdomain has exactly 48 and some exactly 8. `own_rows`: entries r * 4096 to (r+1) * 4096 - 1 name rows of row shard r in local numbering. `send_rows`: entries r * 4096 to (r+1) * 4096 - 1 name rows of row shard r in local numbering.
All inputs are finite; a program needn't handle non-finite values. No bound on the sum of `couple` on one device may be relied on, other than what follows from the above.
Results may differ from the reference program's by a relative error of at most 0.0029.
Values may be sent and summed in bfloat16 or wider, within the bound.
A program may use at most 64 MiB of HBM per device.

```python
import math
import jax
import jax.numpy as jnp
from jax import lax

KMAX = 48
KMIN = 8
NMAT = 16
CX = 2
GY = 16
GZ = 128
SLAB_DEV = 4096
NSUB = 8
GX = 128
N_ROW = 64


def draw_counts(key, part):
    key = jax.random.fold_in(key, 17)
    key_draw, key_order = jax.random.split(key)
    drawn = jax.random.randint(key_draw, (NSUB,), KMIN, KMAX + 1)
    shuffled = jax.random.permutation(key_order, NSUB)
    drawn = drawn.at[shuffled[0]].set(KMAX)
    return drawn.at[shuffled[1]].set(KMIN).astype(jnp.int32)


def place_ends(result, own_key, least, largest):
    longest = result.shape.index(max(result.shape))
    spots = []
    for shift in (0, 1):
        where = [jax.random.randint(jax.random.fold_in(own_key, axis), (), 0, length) for axis, length in enumerate(result.shape)]
        where[longest] = (where[longest] + shift) % result.shape[longest]
        spots.append(tuple(where))
    return result.at[spots[0]].set(least).at[spots[1]].set(largest)


def shard_levels(stream_key, dims, cuts, smallest, top_value):
    level, own = 1.0, jax.random.fold_in(stream_key, 6)
    for axis_at, parts in cuts:
        draws = jnp.exp(jax.random.uniform(jax.random.fold_in(own, axis_at), (parts,), jnp.float32, smallest / len(cuts), top_value / len(cuts)))
        level = level * jnp.repeat(draws, dims[axis_at] // parts).reshape([-1 if axis == axis_at else 1 for axis in range(len(dims))])
    return level


def scatter_about(own_key, extent, spread, reach, cuts=(), kind=jnp.bfloat16):
    gain = shard_levels(own_key, extent, cuts, -0.22, 0.18) if cuts else 1.0
    result = jax.random.normal(own_key, extent, jnp.float32) * spread * gain
    return jnp.minimum(jnp.maximum(result, -reach), reach).astype(kind)


def setup_inputs(seed: int = 0) -> dict:
    arg_keys = jax.random.split(jax.random.key(seed), 8)
    return {
        "eigen_basis": scatter_about(arg_keys[0], (NSUB, KMAX, 3, GX, GY, GZ), 1.0, 6.0, ((0, 8), (3, 64))),
        "material": place_ends(jax.random.randint(arg_keys[1], (NSUB, GX, GY, GZ), 0, NMAT), jax.random.fold_in(arg_keys[1], 1), 0, NMAT - 1).astype(jnp.int32),
        "counts": draw_counts(jax.random.fold_in(arg_keys[7], 71), 0),
        "couple": place_ends((jax.random.randint(arg_keys[3], (NSUB, 2), 0, 4) < 3).astype(jnp.int32), jax.random.fold_in(arg_keys[3], 1), 0, 1),
        "own_rows": place_ends(jax.random.randint(arg_keys[4], (NSUB, 2, N_ROW * SLAB_DEV), 0, 3 * CX * GY * GZ), jax.random.fold_in(arg_keys[4], 1), 0, (3 * CX * GY * GZ) - 1).astype(jnp.int32),
        "send_rows": place_ends(jax.random.randint(arg_keys[5], (NSUB, 2, N_ROW * SLAB_DEV), 0, 3 * CX * GY * GZ), jax.random.fold_in(arg_keys[5], 1), 0, (3 * CX * GY * GZ) - 1).astype(jnp.int32),
        "stiffness": jnp.clip(jnp.exp(jax.random.uniform(arg_keys[6], (NMAT,), jnp.float32, math.log(0.02), math.log(0.2))), 0.02, 0.2),
    }


NORMAL_WEIGHT = 3.0

def lookup_stiffness(material, stiffness):
    summed = jnp.zeros(material.shape, jnp.float32)
    for level in range(stiffness.shape[0]):
        summed = summed + jnp.where(material == level, stiffness[level], jnp.float32(0.0))
    return summed

def face_term(field, stiff, along):
    length = field.shape[along]
    lower = lax.slice_in_dim(field, 0, length - 1, axis=along)
    upper = lax.slice_in_dim(field, 1, length, axis=along)
    coef = 0.5 * (lax.slice_in_dim(stiff, 0, length - 1, axis=along - 2) + lax.slice_in_dim(stiff, 1, length, axis=along - 2))
    flux = coef * (upper - lower)
    pad_low = [(0, 0)] * field.ndim
    pad_high = [(0, 0)] * field.ndim
    pad_low[along] = (1, 0)
    pad_high[along] = (0, 1)
    return jnp.pad(flux, pad_low) - jnp.pad(flux, pad_high)

def component_weight(axis):
    return jnp.where(jnp.arange(3) == axis, NORMAL_WEIGHT, 1.0).reshape(1, 3, 1, 1, 1)

def apply_stencil(masked, stiff):
    field = masked.astype(jnp.float32)
    summed = jnp.zeros(field.shape, jnp.float32)
    for axis in range(3):
        summed = summed + component_weight(axis) * face_term(field, stiff, axis + 2)
    return summed

def to_shards(values):
    shaped = values.reshape(KMAX, 3, N_ROW, CX, GY, GZ).transpose(2, 0, 1, 3, 4, 5)
    return shaped.reshape(N_ROW, KMAX, 3 * CX * GY * GZ)

def pick_rows(shards, indices):
    return jax.vmap(lambda rows_of, which: jnp.take(rows_of, which, axis=1))(shards, indices)

def reference(eigen_basis, material, counts, couple, own_rows, send_rows, stiffness):

    def one_subdomain(items):
        basis_one, material_one, count_one, own_one, send_one = items
        column_mask = (jnp.arange(KMAX) < count_one).astype(jnp.bfloat16)
        masked = basis_one * column_mask[:, None, None, None, None]
        image = apply_stencil(masked, lookup_stiffness(material_one, stiffness)).astype(jnp.bfloat16)
        diagonal_block = jnp.dot(masked.reshape(KMAX, -1), image.reshape(KMAX, -1).T, preferred_element_type=jnp.float32)
        z_shards = to_shards(masked)
        w_shards = to_shards(image)
        own_sel = jnp.stack([pick_rows(z_shards, own_one[offset].reshape(N_ROW, SLAB_DEV)) for offset in range(2)])
        send_sel = jnp.stack([pick_rows(w_shards, send_one[offset].reshape(N_ROW, SLAB_DEV)) for offset in range(2)])
        return (diagonal_block, own_sel, send_sel)
    diagonal_blocks, own_sel, send_sel = lax.map(one_subdomain, (eigen_basis, material, counts, own_rows, send_rows))
    coarse_diag = diagonal_blocks * (1.0 / (3 * GX * GY * GZ))
    scale_off = 1.0 / math.sqrt(N_ROW * SLAB_DEV)
    forward = []
    for offset in range(2):
        peer_slab = jnp.roll(send_sel[:, offset], -(offset + 1), axis=0)
        block = jnp.einsum('irks,irls->ikl', own_sel[:, offset].astype(jnp.float32), peer_slab.astype(jnp.float32))
        factor = couple[:, offset].astype(jnp.float32) * scale_off
        forward.append(block * factor[:, None, None])
    backward = [jnp.roll(forward[offset], offset + 1, axis=0).transpose(0, 2, 1) for offset in range(2)]
    coarse_off = jnp.stack([backward[1], backward[0], forward[0], forward[1]], axis=1)
    return (coarse_diag, coarse_off)
```

```python
import functools
import math

import jax
import jax.numpy as jnp
from jax import lax
from jax.experimental import pallas as pl
from jax.experimental.pallas import tpu as pltpu
from jax.sharding import PartitionSpec as P

MESH = pl.DeviceIdType.MESH
F32 = jnp.float32
BF16 = jnp.bfloat16

K = 48
C = 3
CX = 2
GY = 16
GZ = 128
CELLS = CX * GY * GZ
ROWS = C * CELLS
NSUB = 8
NROW = 64
PLANES = NROW * CX
SLAB = 4096
CHUNK = 1024
NCHUNK = SLAB // CHUNK
NLEVEL = 16
GROUP = 8
OWNERS = 6
LANES = 128
UNROLL = 128


def at_sub(sub, by):
    return lax.rem(sub + (by + NSUB), NSUB)


def start_barrier(sub, row):
    z, place = row // GROUP, lax.rem(row, GROUP)
    barrier = pltpu.get_barrier_semaphore()

    def signal(to_sub, to_row):
        pl.semaphore_signal(barrier, inc=1, device_id=(to_sub, to_row), device_id_type=MESH)

    @pl.when(row > 0)
    def _():
        signal(sub, row - 1)

    @pl.when(row < NROW - 1)
    def _():
        signal(sub, row + 1)

    for by in (1, 2):
        signal(at_sub(sub, -by), row)
        for q in range(OWNERS):
            signal(at_sub(sub, by), z * GROUP + q)
    for step in range(1, GROUP):
        signal(sub, z * GROUP + lax.rem(place + step, GROUP))

    @pl.when(place < OWNERS)
    def _():
        for step in range(1, 8):
            signal(sub, lax.rem(z + step, 8) * GROUP + place)

    owner = (place < OWNERS).astype(jnp.int32)
    sides = (row > 0).astype(jnp.int32) + (row < NROW - 1).astype(jnp.int32)
    return barrier, sides + 2 + (GROUP - 1) + owner * (7 + 2 * GROUP)


def gather(index_of, table, dest, first, count):
    def body(step, carry):
        base = pl.multiple_of(step * UNROLL, UNROLL)
        for u in range(UNROLL):
            dest[pl.ds(base + u, 1), :] = table[pl.ds(index_of(first + base + u), 1), :]
        return carry

    lax.fori_loop(0, count // UNROLL, body, 0)


def widen(tile):
    return jnp.concatenate([tile, jnp.zeros((GZ, LANES - K), F32)], axis=1)


def kernel(
    counts, couple, stiffness, eigen, material, own_rows, send_rows,
    diag_out, off_out,
    eig, halo, mat, coef, field, image, table, own_sel, send_sel, packed, arrived,
    own_index, send_index, part, sums, zsums, piece, whole, forward,
    load_sem, halo_send, halo_recv, slab_send, slab_recv,
    one_send, one_recv, two_send, two_recv, three_send, three_recv, fwd_send, fwd_recv,
):
    sub, row = lax.axis_index("sub"), lax.axis_index("row")
    z, place = row // GROUP, lax.rem(row, GROUP)
    barrier, greetings = start_barrier(sub, row)

    loads = [pltpu.make_async_copy(eigen.at[0], eig, load_sem.at[0])]
    loads.append(pltpu.make_async_copy(own_rows, own_index, load_sem.at[1]))
    loads.append(pltpu.make_async_copy(send_rows, send_index, load_sem.at[2]))
    for p in range(CX + 2):
        plane = jnp.clip(row * CX + (p - 1), 0, PLANES - 1)
        loads.append(pltpu.make_async_copy(material.at[0, plane], mat.at[p], load_sem.at[3 + p]))
    for load in loads:
        load.start()

    count = counts[0]

    def kept(k):
        return (k < count).astype(F32)

    loads[0].wait()

    pl.semaphore_wait(barrier, greetings)
    up = pltpu.make_async_remote_copy(
        src_ref=eig.at[:, :, CX - 1], dst_ref=halo.at[0], send_sem=halo_send.at[0],
        recv_sem=halo_recv.at[0], device_id=(sub, jnp.minimum(row + 1, NROW - 1)), device_id_type=MESH)
    down = pltpu.make_async_remote_copy(
        src_ref=eig.at[:, :, 0], dst_ref=halo.at[1], send_sem=halo_send.at[1],
        recv_sem=halo_recv.at[1], device_id=(sub, jnp.maximum(row - 1, 0)), device_id_type=MESH)

    @pl.when(row < NROW - 1)
    def _():
        up.start()

    @pl.when(row > 0)
    def _():
        down.start()

    @pl.when(row == 0)
    def _():
        halo[0] = jnp.zeros((K, C, GY, GZ), BF16)

    @pl.when(row == NROW - 1)
    def _():
        halo[1] = jnp.zeros((K, C, GY, GZ), BF16)

    def mask_column(k, carry):
        keep = kept(k)
        for c in range(C):
            for p in range(CX):
                base = pl.multiple_of(k * (C * CX * GY) + (c * CX + p) * GY, GY)
                field[pl.ds(base, GY), :] = eig[k, c, p].astype(F32) * keep
        return carry

    lax.fori_loop(0, K, mask_column, 0)

    def across(source, at):
        return source[pl.ds(at, K, stride=C * CX * GY), :]

    def fill_table(at, carry):
        table[pl.ds(pl.multiple_of(at * GZ, GZ), GZ), :] = widen(across(field, at).T)
        return carry

    lax.fori_loop(0, C * CX * GY, fill_table, 0)

    loads[1].wait()
    lane = lax.broadcasted_iota(jnp.int32, (K, LANES), 1)
    line = lax.broadcasted_iota(jnp.int32, (K, LANES), 0)
    slabs = []
    for o in (1, 0):
        turn = jnp.where(lane == line, couple[0, o].astype(F32), F32(0)).astype(BF16)
        for n in range(NCHUNK):
            gather(lambda t: own_index[0, o, t], table, own_sel, n * CHUNK, CHUNK)

            def turned(step, carry):
                base = pl.multiple_of(step * 256, 256)
                picked = own_sel[pl.ds(base, 256), :].astype(BF16)
                packed[o, n, :, pl.ds(base, 256)] = lax.dot_general(
                    turn, picked, (((1,), (1,)), ((), ())), preferred_element_type=F32).astype(BF16)
                return carry

            lax.fori_loop(0, CHUNK // 256, turned, 0)
            slab = pltpu.make_async_remote_copy(
                src_ref=packed.at[o, n], dst_ref=arrived.at[o, n],
                send_sem=slab_send.at[o, n], recv_sem=slab_recv.at[o, n],
                device_id=(at_sub(sub, o + 1), row), device_id_type=MESH)
            slab.start()
            slabs.append(slab)

    for p in range(CX + 2):
        loads[3 + p].wait()
    kappa = []
    for p in range(CX + 2):
        level = mat[p]
        found = jnp.zeros((GY, GZ), F32)
        for m in range(NLEVEL):
            found = found + jnp.where(level == m, stiffness[m], F32(0))
        kappa.append(found)
    for p in range(CX + 1):
        face = 0.5 * (kappa[p] + kappa[p + 1])
        if p == 0:
            face = face * (row > 0).astype(F32)
        if p == CX:
            face = face * (row < NROW - 1).astype(F32)
        coef[p] = face
    in_y = lax.broadcasted_iota(jnp.int32, (GY, GZ), 0) < GY - 1
    in_z = lax.broadcasted_iota(jnp.int32, (GY, GZ), 1) < GZ - 1
    for p in range(CX):
        mid = kappa[p + 1]
        coef[CX + 1 + p] = jnp.where(in_y, 0.5 * (mid + pltpu.roll(mid, GY - 1, 0)), 0.0)
        coef[2 * CX + 1 + p] = jnp.where(in_z, 0.5 * (mid + pltpu.roll(mid, GZ - 1, 1)), 0.0)

    @pl.when(row > 0)
    def _():
        up.wait_recv()

    @pl.when(row < NROW - 1)
    def _():
        down.wait_recv()

    def apply_column(k, carry):
        keep = kept(k)
        for c in range(C):
            def at(p):
                return pl.multiple_of(k * (C * CX * GY) + (c * CX + p) * GY, GY)

            cells = [halo[0, k, c].astype(F32) * keep]
            cells += [field[pl.ds(at(p), GY), :] for p in range(CX)]
            cells.append(halo[1, k, c].astype(F32) * keep)
            flux = [coef[p] * (cells[p + 1] - cells[p]) for p in range(CX + 1)]
            for p in range(CX):
                u = cells[p + 1]
                term_x = flux[p] - flux[p + 1]
                flux_y = coef[CX + 1 + p] * (pltpu.roll(u, GY - 1, 0) - u)
                term_y = pltpu.roll(flux_y, 1, 0) - flux_y
                flux_z = coef[2 * CX + 1 + p] * (pltpu.roll(u, GZ - 1, 1) - u)
                term_z = pltpu.roll(flux_z, 1, 1) - flux_z
                terms = [term_x, term_y, term_z]
                terms[c] = 3.0 * terms[c]
                total = terms[0] + terms[1] + terms[2]
                image[pl.ds(at(p), GY), :] = total.astype(BF16).astype(F32)
        return carry

    lax.fori_loop(0, K, apply_column, 0)

    def image_table(at, total):
        turned = widen(across(image, at).T)
        table[pl.ds(pl.multiple_of(at * GZ, GZ), GZ), :] = turned
        return total + jnp.dot(
            across(field, at).astype(BF16), turned.astype(BF16), preferred_element_type=F32)

    diag = lax.fori_loop(0, C * CX * GY, image_table, jnp.zeros((K, LANES), F32))

    loads[2].wait()
    for o in (1, 0):
        gather(lambda t: send_index[0, o, t], table, send_sel.at[o], 0, SLAB)

    mats = [diag]
    for o in (0, 1):
        for n in range(NCHUNK):
            slabs[(1 - o) * NCHUNK + n].wait_recv()

        def multiply(step, total, o=o):
            n = step
            picked = send_sel[o, pl.ds(pl.multiple_of(n * CHUNK, CHUNK), CHUNK), :].astype(BF16)
            return total + jnp.dot(arrived[o, n], picked, preferred_element_type=F32)

        mats.append(lax.fori_loop(0, NCHUNK, multiply, jnp.zeros((K, LANES), F32)))
    for q in range(OWNERS):
        for m in range(3):
            part[q, pl.ds(8 * m, 8), :] = mats[m][8 * q : 8 * q + 8]

    is_owner = place < OWNERS
    firsts = []
    for step in range(1, GROUP):
        to = lax.rem(place + step, GROUP)
        to_q = jnp.minimum(to, OWNERS - 1)
        firsts.append((to, pltpu.make_async_remote_copy(
            src_ref=part.at[to_q], dst_ref=sums.at[place],
            send_sem=one_send.at[step], recv_sem=one_recv.at[place],
            device_id=(sub, z * GROUP + to), device_id_type=MESH)))
    for to, copy in firsts:
        @pl.when(to < OWNERS)
        def _(copy=copy):
            copy.start()

    seconds = []
    for step in range(1, 8):
        seconds.append(pltpu.make_async_remote_copy(
            src_ref=piece.at[0], dst_ref=zsums.at[z],
            send_sem=two_send.at[step], recv_sem=two_recv.at[z],
            device_id=(sub, lax.rem(z + step, 8) * GROUP + place), device_id_type=MESH))

    thirds = []
    own_q = jnp.minimum(place, OWNERS - 1)
    for step in range(1, GROUP):
        thirds.append(pltpu.make_async_remote_copy(
            src_ref=piece.at[1], dst_ref=whole.at[own_q],
            send_sem=three_send.at[step], recv_sem=three_recv.at[own_q],
            device_id=(sub, z * GROUP + lax.rem(place + step, GROUP)), device_id_type=MESH))
    for o in (0, 1):
        for to in range(GROUP):
            thirds.append(pltpu.make_async_remote_copy(
                src_ref=piece.at[1, pl.ds(8 + 8 * o, 8)], dst_ref=forward.at[o, own_q],
                send_sem=fwd_send.at[o, to], recv_sem=fwd_recv.at[o, own_q],
                device_id=(at_sub(sub, -o - 1), z * GROUP + to), device_id_type=MESH))

    @pl.when(is_owner)
    def _():
        for step in range(1, GROUP):
            source = lax.rem(place + step, GROUP)
            pltpu.make_async_remote_copy(
                src_ref=part.at[0], dst_ref=sums.at[source], send_sem=one_send.at[step],
                recv_sem=one_recv.at[source], device_id=(sub, row), device_id_type=MESH).wait_recv()
        total = part[own_q]
        for step in range(1, GROUP):
            total = total + sums[lax.rem(place + step, GROUP)]
        piece[0] = total
        for copy in seconds:
            copy.start()
        for step in range(1, 8):
            source = lax.rem(z + step, 8)
            pltpu.make_async_remote_copy(
                src_ref=piece.at[0], dst_ref=zsums.at[source], send_sem=two_send.at[step],
                recv_sem=two_recv.at[source], device_id=(sub, row), device_id_type=MESH).wait_recv()
        for step in range(1, 8):
            total = total + zsums[lax.rem(z + step, 8)]
        piece[1] = total
        for copy in thirds:
            copy.start()
        whole[own_q] = total

    for q in range(OWNERS):
        @pl.when(place != q)
        def _(q=q):
            pltpu.make_async_remote_copy(
                src_ref=piece.at[1], dst_ref=whole.at[q], send_sem=three_send.at[0],
                recv_sem=three_recv.at[q], device_id=(sub, row), device_id_type=MESH).wait_recv()
        for o in (0, 1):
            pltpu.make_async_remote_copy(
                src_ref=piece.at[1, pl.ds(8, 8)], dst_ref=forward.at[o, q], send_sem=fwd_send.at[o, q],
                recv_sem=fwd_recv.at[o, q], device_id=(sub, row), device_id_type=MESH).wait_recv()

    scale = 1.0 / math.sqrt(NROW * SLAB)
    diag_out[0] = jnp.concatenate([whole[q, 0:8, :K] for q in range(OWNERS)], axis=0) * (1.0 / (C * PLANES * GY * GZ))
    for o in (0, 1):
        pair = jnp.concatenate([whole[q, 8 + 8 * o : 16 + 8 * o, :] for q in range(OWNERS)], axis=0)
        off_out[0, 1 - o] = pair.T[:K, :] * scale
        off_out[0, 2 + o] = jnp.concatenate([forward[o, q, :, :K] for q in range(OWNERS)], axis=0) * scale

    @pl.when(row < NROW - 1)
    def _():
        up.wait_send()

    @pl.when(row > 0)
    def _():
        down.wait_send()

    for slab in slabs:
        slab.wait_send()
    for to, copy in firsts:
        @pl.when(to < OWNERS)
        def _(copy=copy):
            copy.wait_send()

    @pl.when(is_owner)
    def _():
        for copy in seconds + thirds:
            copy.wait_send()


def shards(eigen_basis, material, counts, couple, own_rows, send_rows, stiffness):
    smem = pl.BlockSpec(memory_space=pltpu.SMEM)
    anywhere = pl.BlockSpec(memory_space=pl.ANY)
    vmem = pl.BlockSpec(memory_space=pltpu.VMEM)
    dma = pltpu.SemaphoreType.DMA
    return pl.pallas_call(
        kernel,
        out_shape=(jax.ShapeDtypeStruct((1, K, K), F32), jax.ShapeDtypeStruct((1, 4, K, K), F32)),
        in_specs=[smem, smem, smem, anywhere, anywhere, anywhere, anywhere],
        out_specs=(vmem, vmem),
        scratch_shapes=[
            pltpu.VMEM((K, C, CX, GY, GZ), BF16),
            pltpu.VMEM((2, K, C, GY, GZ), BF16),
            pltpu.VMEM((CX + 2, GY, GZ), jnp.int32),
            pltpu.VMEM((3 * CX + 1, GY, GZ), F32),
            pltpu.VMEM((K * C * CX * GY, GZ), F32),
            pltpu.VMEM((K * C * CX * GY, GZ), F32),
            pltpu.VMEM((ROWS, LANES), F32),
            pltpu.VMEM((CHUNK, LANES), F32),
            pltpu.VMEM((2, SLAB, LANES), F32),
            pltpu.VMEM((2, NCHUNK, K, CHUNK), BF16),
            pltpu.VMEM((2, NCHUNK, K, CHUNK), BF16),
            pltpu.SMEM((1, 2, SLAB), jnp.int32),
            pltpu.SMEM((1, 2, SLAB), jnp.int32),
            pltpu.VMEM((OWNERS, 24, LANES), F32),
            pltpu.VMEM((GROUP, 24, LANES), F32),
            pltpu.VMEM((8, 24, LANES), F32),
            pltpu.VMEM((2, 24, LANES), F32),
            pltpu.VMEM((OWNERS, 24, LANES), F32),
            pltpu.VMEM((2, OWNERS, 8, LANES), F32),
            dma((3 + CX + 2,)), dma((2,)), dma((2,)), dma((2, NCHUNK)), dma((2, NCHUNK)),
            dma((GROUP,)), dma((GROUP,)), dma((8,)), dma((8,)),
            dma((GROUP,)), dma((OWNERS,)), dma((2, GROUP)), dma((2, OWNERS)),
        ],
        compiler_params=pltpu.CompilerParams(
            collective_id=0, has_side_effects=True, vmem_limit_bytes=48 * 2**20),
        name="coarse",
    )(counts, couple, stiffness, eigen_basis, material, own_rows, send_rows)


def solution(mesh):
    in_specs = (
        P("sub", None, None, "row", None, None),
        P("sub", None, None, None),
        P("sub"),
        P("sub", None),
        P("sub", None, "row"),
        P("sub", None, "row"),
        P(),
    )
    out_specs = (P("sub", None, None), P("sub", None, None, None))
    return jax.shard_map(shards, mesh=mesh, in_specs=in_specs, out_specs=out_specs, check_vma=False)
```

```python
import functools
import math

import jax
import jax.numpy as jnp
from jax import lax
from jax.experimental import pallas as pl
from jax.experimental.pallas import tpu as pltpu
from jax.sharding import PartitionSpec as P

MESH = pl.DeviceIdType.MESH
F32 = jnp.float32
BF16 = jnp.bfloat16

K = 48
C = 3
CX = 2
GY = 16
GZ = 128
CELLS = CX * GY * GZ
ROWS = C * CELLS
NSUB = 8
NROW = 64
PLANES = NROW * CX
SLAB = 4096
CHUNK = 1024
NCHUNK = SLAB // CHUNK
NLEVEL = 16
GROUP = 8
OWNERS = 6
LANES = 128
STRIPS = 8
STEP = 8
STRIP = SLAB // STRIPS


def at_sub(sub, by):
    return lax.rem(sub + (by + NSUB), NSUB)


def start_barrier(sub, row):
    z, place = row // GROUP, lax.rem(row, GROUP)
    barrier = pltpu.get_barrier_semaphore()

    def signal(to_sub, to_row):
        pl.semaphore_signal(barrier, inc=1, device_id=(to_sub, to_row), device_id_type=MESH)

    @pl.when(row > 0)
    def _():
        signal(sub, row - 1)

    @pl.when(row < NROW - 1)
    def _():
        signal(sub, row + 1)

    for by in (1, 2):
        signal(at_sub(sub, -by), row)
        for q in range(OWNERS):
            signal(at_sub(sub, by), z * GROUP + q)
    for step in range(1, GROUP):
        signal(sub, z * GROUP + lax.rem(place + step, GROUP))

    @pl.when(place < OWNERS)
    def _():
        for step in range(1, 8):
            signal(sub, lax.rem(z + step, 8) * GROUP + place)

    owner = (place < OWNERS).astype(jnp.int32)
    sides = (row > 0).astype(jnp.int32) + (row < NROW - 1).astype(jnp.int32)
    return barrier, sides + 2 + (GROUP - 1) + owner * (7 + 2 * GROUP)


def gather(index, table, dest, first, count):
    def body(step, carry):
        base = pl.multiple_of(step * (STRIPS * STEP), STRIPS * STEP)
        at = first // STRIPS + step * STEP
        for q in range(STRIPS):
            for j in range(STEP):
                dest[pl.ds(base + (q * STEP + j), 1), :] = table[pl.ds(index[q][at + j], 1), :]
        return carry

    lax.fori_loop(0, count // (STRIPS * STEP), body, 0)


def widen(tile):
    return jnp.concatenate([tile, jnp.zeros((GZ, LANES - K), F32)], axis=1)


def kernel(
    counts_in, couple_in, stiffness_in, eigen, material, own_rows, send_rows,
    diag_out, off_out,
    counts, couple, stiffness, eig, halo, mat, coef, field, image, table, own_sel, send_sel, packed, arrived,
    part, sums, zsums, piece, whole, forward,
    load_sem, halo_send, halo_recv, slab_send, slab_recv,
    one_send, one_recv, two_send, two_recv, three_send, three_recv, fwd_send, fwd_recv, index_sem, *strips,
):
    sub, row = lax.axis_index("sub"), lax.axis_index("row")
    z, place = row // GROUP, lax.rem(row, GROUP)
    barrier, greetings = start_barrier(sub, row)

    loads = [pltpu.make_async_copy(eigen.at[0], eig, load_sem.at[0])]
    own_index = [strips[o * STRIPS : (o + 1) * STRIPS] for o in (0, 1)]
    send_index = [strips[(2 + o) * STRIPS : (3 + o) * STRIPS] for o in (0, 1)]
    index_loads = []
    for kind, (rows, index) in enumerate(((own_rows, own_index), (send_rows, send_index))):
        index_loads.append([])
        for o in (1, 0):
            for q in range(STRIPS):
                index_loads[kind].append(pltpu.make_async_copy(
                    rows.at[0, o, pl.ds(q * STRIP, STRIP)], index[o][q], index_sem.at[kind, o, q]))
    for p in range(CX + 2):
        plane = jnp.clip(row * CX + (p - 1), 0, PLANES - 1)
        loads.append(pltpu.make_async_copy(material.at[0, plane], mat.at[p], load_sem.at[1 + p]))
    loads.append(pltpu.make_async_copy(counts_in, counts, load_sem.at[3 + CX]))
    loads.append(pltpu.make_async_copy(couple_in, couple, load_sem.at[4 + CX]))
    loads.append(pltpu.make_async_copy(stiffness_in, stiffness, load_sem.at[5 + CX]))
    for load in loads + index_loads[0] + index_loads[1]:
        load.start()
    loads[3 + CX].wait()
    count = counts[0]

    def kept(k):
        return (k < count).astype(F32)

    pl.semaphore_wait(barrier, greetings)
    up = pltpu.make_async_remote_copy(
        src_ref=eigen.at[0, :, :, CX - 1], dst_ref=halo.at[0], send_sem=halo_send.at[0],
        recv_sem=halo_recv.at[0], device_id=(sub, jnp.minimum(row + 1, NROW - 1)), device_id_type=MESH)
    down = pltpu.make_async_remote_copy(
        src_ref=eigen.at[0, :, :, 0], dst_ref=halo.at[1], send_sem=halo_send.at[1],
        recv_sem=halo_recv.at[1], device_id=(sub, jnp.maximum(row - 1, 0)), device_id_type=MESH)

    @pl.when(row < NROW - 1)
    def _():
        up.start()

    @pl.when(row > 0)
    def _():
        down.start()

    @pl.when(row == 0)
    def _():
        halo[0] = jnp.zeros((K, C, GY, GZ), BF16)

    @pl.when(row == NROW - 1)
    def _():
        halo[1] = jnp.zeros((K, C, GY, GZ), BF16)

    loads[0].wait()

    def mask_column(k, carry):
        keep = kept(k)
        for c in range(C):
            for p in range(CX):
                base = pl.multiple_of(k * (C * CX * GY) + (c * CX + p) * GY, GY)
                field[pl.ds(base, GY), :] = eig[k, c, p].astype(F32) * keep
        return carry

    lax.fori_loop(0, K, mask_column, 0)

    def across(source, at):
        return source[pl.ds(at, K, stride=C * CX * GY), :]

    def fill_table(block, carry):
        for y in range(GY):
            at = block * GY + y
            table[pl.ds(pl.multiple_of(at * GZ, GZ), GZ), :] = widen(across(field, at).T)
        return carry

    lax.fori_loop(0, C * CX, fill_table, 0)

    for load in index_loads[0]:
        load.wait()
    loads[4 + CX].wait()
    lane = lax.broadcasted_iota(jnp.int32, (K, LANES), 1)
    line = lax.broadcasted_iota(jnp.int32, (K, LANES), 0)
    slabs = []
    for o in (1, 0):
        turn = jnp.where(lane == line, couple[0, o].astype(F32), F32(0)).astype(BF16)
        for n in range(NCHUNK):
            gather(own_index[o], table, own_sel, n * CHUNK, CHUNK)

            for base in range(0, CHUNK, 256):
                picked = own_sel[pl.ds(base, 256), :].astype(BF16)
                packed[o, n, :, pl.ds(base, 256)] = lax.dot_general(
                    turn, picked, (((1,), (1,)), ((), ())), preferred_element_type=F32).astype(BF16)
            slab = pltpu.make_async_remote_copy(
                src_ref=packed.at[o, n], dst_ref=arrived.at[o, n],
                send_sem=slab_send.at[o, n], recv_sem=slab_recv.at[o, n],
                device_id=(at_sub(sub, o + 1), row), device_id_type=MESH)
            slab.start()
            slabs.append(slab)

    for p in range(CX + 2):
        loads[1 + p].wait()
    loads[5 + CX].wait()
    kappa = []
    for p in range(CX + 2):
        level = mat[p]
        found = jnp.zeros((GY, GZ), F32)
        for m in range(NLEVEL):
            found = found + jnp.where(level == m, stiffness[m], F32(0))
        kappa.append(found)
    faces = []
    for p in range(CX + 1):
        face = 0.5 * (kappa[p] + kappa[p + 1])
        if p == 0:
            face = face * (row > 0).astype(F32)
        if p == CX:
            face = face * (row < NROW - 1).astype(F32)
        coef[p] = face
        faces.append(face)
    in_y = lax.broadcasted_iota(jnp.int32, (GY, GZ), 0) < GY - 1
    in_z = lax.broadcasted_iota(jnp.int32, (GY, GZ), 1) < GZ - 1
    for p in range(CX):
        mid = kappa[p + 1]
        y_up = jnp.where(in_y, 0.5 * (mid + pltpu.roll(mid, GY - 1, 0)), 0.0)
        z_up = jnp.where(in_z, 0.5 * (mid + pltpu.roll(mid, GZ - 1, 1)), 0.0)
        y_down, z_down = pltpu.roll(y_up, 1, 0), pltpu.roll(z_up, 1, 1)
        for n, face in enumerate((y_down, y_up, z_down, z_up)):
            coef[CX + 1 + 4 * p + n] = face
        along = (faces[p] + faces[p + 1], y_down + y_up, z_down + z_up)
        for c in range(C):
            coef[5 * CX + 1 + C * p + c] = along[0] + along[1] + along[2] + 2.0 * along[c]

    @pl.when(row > 0)
    def _():
        up.wait_recv()

    @pl.when(row < NROW - 1)
    def _():
        down.wait_recv()

    def apply_column(k):
        keep = kept(k)
        for c in range(C):
            def at(p):
                return pl.multiple_of(k * (C * CX * GY) + (c * CX + p) * GY, GY)

            cells = [halo[0, k, c].astype(F32) * keep]
            cells += [field[pl.ds(at(p), GY), :] for p in range(CX)]
            cells.append(halo[1, k, c].astype(F32) * keep)
            for p in range(CX):
                u = cells[p + 1]
                face = [coef[CX + 1 + 4 * p + n] for n in range(4)]
                near = [
                    coef[p] * cells[p] + coef[p + 1] * cells[p + 2],
                    face[0] * pltpu.roll(u, 1, 0) + face[1] * pltpu.roll(u, GY - 1, 0),
                    face[2] * pltpu.roll(u, 1, 1) + face[3] * pltpu.roll(u, GZ - 1, 1),
                ]
                own = coef[5 * CX + 1 + C * p + c]
                image[pl.ds(at(p), GY), :] = own * u - (near[0] + near[1] + near[2] + 2.0 * near[c])

    def apply_columns(block, carry):
        for u in range(4):
            apply_column(4 * block + u)
        return carry

    lax.fori_loop(0, K // 4, apply_columns, 0)

    def image_table(block, total):
        basis, turned = [], []
        for y in range(GY):
            at = block * GY + y
            wide = widen(across(image, at).T)
            table[pl.ds(pl.multiple_of(at * GZ, GZ), GZ), :] = wide
            turned.append(wide.astype(BF16))
            basis.append(across(field, at).astype(BF16))
        return total + jnp.dot(
            jnp.concatenate(basis, axis=1), jnp.concatenate(turned, axis=0), preferred_element_type=F32)

    diag = lax.fori_loop(0, C * CX, image_table, jnp.zeros((K, LANES), F32))

    for load in index_loads[1]:
        load.wait()
    for o in (1, 0):
        gather(send_index[o], table, send_sel.at[o], 0, SLAB)

    mats = [diag]
    for o in (0, 1):
        for n in range(NCHUNK):
            slabs[(1 - o) * NCHUNK + n].wait_recv()

        def multiply(step, total, o=o):
            n = step
            picked = send_sel[o, pl.ds(pl.multiple_of(n * CHUNK, CHUNK), CHUNK), :].astype(BF16)
            return total + jnp.dot(arrived[o, n], picked, preferred_element_type=F32)

        mats.append(lax.fori_loop(0, NCHUNK, multiply, jnp.zeros((K, LANES), F32)))
    for q in range(OWNERS):
        for m in range(3):
            part[q, pl.ds(8 * m, 8), :] = mats[m][8 * q : 8 * q + 8]

    is_owner = place < OWNERS
    firsts = []
    for step in range(1, GROUP):
        to = lax.rem(place + step, GROUP)
        to_q = jnp.minimum(to, OWNERS - 1)
        firsts.append((to, pltpu.make_async_remote_copy(
            src_ref=part.at[to_q], dst_ref=sums.at[place],
            send_sem=one_send.at[step], recv_sem=one_recv.at[place],
            device_id=(sub, z * GROUP + to), device_id_type=MESH)))
    for to, copy in firsts:
        @pl.when(to < OWNERS)
        def _(copy=copy):
            copy.start()

    seconds = []
    for step in range(1, 8):
        seconds.append(pltpu.make_async_remote_copy(
            src_ref=piece.at[0], dst_ref=zsums.at[z],
            send_sem=two_send.at[step], recv_sem=two_recv.at[z],
            device_id=(sub, lax.rem(z + step, 8) * GROUP + place), device_id_type=MESH))

    thirds = []
    own_q = jnp.minimum(place, OWNERS - 1)
    for step in range(1, GROUP):
        thirds.append(pltpu.make_async_remote_copy(
            src_ref=piece.at[1], dst_ref=whole.at[own_q],
            send_sem=three_send.at[step], recv_sem=three_recv.at[own_q],
            device_id=(sub, z * GROUP + lax.rem(place + step, GROUP)), device_id_type=MESH))
    for o in (0, 1):
        for to in range(GROUP):
            thirds.append(pltpu.make_async_remote_copy(
                src_ref=piece.at[1, pl.ds(8 + 8 * o, 8)], dst_ref=forward.at[o, own_q],
                send_sem=fwd_send.at[o, to], recv_sem=fwd_recv.at[o, own_q],
                device_id=(at_sub(sub, -o - 1), z * GROUP + to), device_id_type=MESH))

    @pl.when(is_owner)
    def _():
        for step in range(1, GROUP):
            source = lax.rem(place + step, GROUP)
            pltpu.make_async_remote_copy(
                src_ref=part.at[0], dst_ref=sums.at[source], send_sem=one_send.at[step],
                recv_sem=one_recv.at[source], device_id=(sub, row), device_id_type=MESH).wait_recv()
        total = part[own_q]
        for step in range(1, GROUP):
            total = total + sums[lax.rem(place + step, GROUP)]
        piece[0] = total
        for copy in seconds:
            copy.start()
        for step in range(1, 8):
            source = lax.rem(z + step, 8)
            pltpu.make_async_remote_copy(
                src_ref=piece.at[0], dst_ref=zsums.at[source], send_sem=two_send.at[step],
                recv_sem=two_recv.at[source], device_id=(sub, row), device_id_type=MESH).wait_recv()
        for step in range(1, 8):
            total = total + zsums[lax.rem(z + step, 8)]
        piece[1] = total
        for copy in thirds:
            copy.start()
        whole[own_q] = total

    for q in range(OWNERS):
        @pl.when(place != q)
        def _(q=q):
            pltpu.make_async_remote_copy(
                src_ref=piece.at[1], dst_ref=whole.at[q], send_sem=three_send.at[0],
                recv_sem=three_recv.at[q], device_id=(sub, row), device_id_type=MESH).wait_recv()
        for o in (0, 1):
            pltpu.make_async_remote_copy(
                src_ref=piece.at[1, pl.ds(8, 8)], dst_ref=forward.at[o, q], send_sem=fwd_send.at[o, q],
                recv_sem=fwd_recv.at[o, q], device_id=(sub, row), device_id_type=MESH).wait_recv()

    scale = 1.0 / math.sqrt(NROW * SLAB)
    diag_out[0] = jnp.concatenate([whole[q, 0:8, :K] for q in range(OWNERS)], axis=0) * (1.0 / (C * PLANES * GY * GZ))
    for o in (0, 1):
        pair = jnp.concatenate([whole[q, 8 + 8 * o : 16 + 8 * o, :] for q in range(OWNERS)], axis=0)
        off_out[0, 1 - o] = pair.T[:K, :] * scale
        off_out[0, 2 + o] = jnp.concatenate([forward[o, q, :, :K] for q in range(OWNERS)], axis=0) * scale

    @pl.when(row < NROW - 1)
    def _():
        up.wait_send()

    @pl.when(row > 0)
    def _():
        down.wait_send()

    for slab in slabs:
        slab.wait_send()
    for to, copy in firsts:
        @pl.when(to < OWNERS)
        def _(copy=copy):
            copy.wait_send()

    @pl.when(is_owner)
    def _():
        for copy in seconds + thirds:
            copy.wait_send()


def shards(eigen_basis, material, counts, couple, own_rows, send_rows, stiffness):
    hbm = pl.BlockSpec(memory_space=pltpu.HBM)
    vmem = pl.BlockSpec(memory_space=pltpu.VMEM)
    dma = pltpu.SemaphoreType.DMA
    return pl.pallas_call(
        kernel,
        out_shape=(jax.ShapeDtypeStruct((1, K, K), F32), jax.ShapeDtypeStruct((1, 4, K, K), F32)),
        in_specs=[hbm] * 7,
        out_specs=(vmem, vmem),
        scratch_shapes=[
            pltpu.SMEM((1,), jnp.int32),
            pltpu.SMEM((1, 2), jnp.int32),
            pltpu.SMEM((NLEVEL,), F32),
            pltpu.VMEM((K, C, CX, GY, GZ), BF16),
            pltpu.VMEM((2, K, C, GY, GZ), BF16),
            pltpu.VMEM((CX + 2, GY, GZ), jnp.int32),
            pltpu.VMEM((5 * CX + 1 + C * CX, GY, GZ), F32),
            pltpu.VMEM((K * C * CX * GY, GZ), F32),
            pltpu.VMEM((K * C * CX * GY, GZ), F32),
            pltpu.VMEM((ROWS, LANES), F32),
            pltpu.VMEM((CHUNK, LANES), F32),
            pltpu.VMEM((2, SLAB, LANES), F32),
            pltpu.VMEM((2, NCHUNK, K, CHUNK), BF16),
            pltpu.VMEM((2, NCHUNK, K, CHUNK), BF16),
            pltpu.VMEM((OWNERS, 24, LANES), F32),
            pltpu.VMEM((GROUP, 24, LANES), F32),
            pltpu.VMEM((8, 24, LANES), F32),
            pltpu.VMEM((2, 24, LANES), F32),
            pltpu.VMEM((OWNERS, 24, LANES), F32),
            pltpu.VMEM((2, OWNERS, 8, LANES), F32),
            dma((6 + CX,)), dma((2,)), dma((2,)), dma((2, NCHUNK)), dma((2, NCHUNK)),
            dma((GROUP,)), dma((GROUP,)), dma((8,)), dma((8,)),
            dma((GROUP,)), dma((OWNERS,)), dma((2, GROUP)), dma((2, OWNERS)),
            dma((2, 2, STRIPS)),
        ] + [pltpu.SMEM((STRIP,), jnp.int32) for _ in range(4 * STRIPS)],
        compiler_params=pltpu.CompilerParams(
            collective_id=0, has_side_effects=True, vmem_limit_bytes=60 * 2**20),
        name="coarse",
    )(counts, couple, stiffness, eigen_basis, material, own_rows, send_rows)


def solution(mesh):
    in_specs = (
        P("sub", None, None, "row", None, None),
        P("sub", None, None, None),
        P("sub"),
        P("sub", None),
        P("sub", None, "row"),
        P("sub", None, "row"),
        P(),
    )
    out_specs = (P("sub", None, None), P("sub", None, None, None))
    return jax.shard_map(shards, mesh=mesh, in_specs=in_specs, out_specs=out_specs, check_vma=False)
```

```python
import functools
import math

import jax
import jax.numpy as jnp
from jax import lax
from jax.experimental import pallas as pl
from jax.experimental.pallas import tpu as pltpu
from jax.sharding import PartitionSpec as P

MESH = pl.DeviceIdType.MESH
F32 = jnp.float32
BF16 = jnp.bfloat16

K = 48
C = 3
CX = 2
GY = 16
GZ = 128
CELLS = CX * GY * GZ
ROWS = C * CELLS
NSUB = 8
NROW = 64
PLANES = NROW * CX
SLAB = 4096
CHUNK = 512
NCHUNK = SLAB // CHUNK
BACK = 3
UP = [(1, n) for n in range(NCHUNK - BACK)] + [(0, n) for n in range(NCHUNK)]
DOWN = [(1, n) for n in range(NCHUNK - BACK, NCHUNK)]
FAR_FIRST = (4, 3, 5, 2, 6, 1, 7)
NLEVEL = 16
GROUP = 8
OWNERS = 6
LANES = 128
STRIPS = 8
STEP = 8
STRIP = SLAB // STRIPS


def at_sub(sub, by):
    return lax.rem(sub + (by + NSUB), NSUB)


def start_barrier(sub, row):
    z, place = row // GROUP, lax.rem(row, GROUP)
    barrier = pltpu.get_barrier_semaphore()

    def signal(to_sub, to_row):
        pl.semaphore_signal(barrier, inc=1, device_id=(to_sub, to_row), device_id_type=MESH)

    @pl.when(row > 0)
    def _():
        signal(sub, row - 1)

    @pl.when(row < NROW - 1)
    def _():
        signal(sub, row + 1)

    for by in (-1, -2, 2):
        signal(at_sub(sub, by), row)
    for step in FAR_FIRST:
        signal(sub, z * GROUP + lax.rem(place + step, GROUP))

    @pl.when(place < OWNERS)
    def _():
        for step in FAR_FIRST:
            signal(sub, lax.rem(z + step, 8) * GROUP + place)

    for by in (2, -2, 1):
        for q in range(OWNERS):
            signal(at_sub(sub, by), z * GROUP + q)

    owner = (place < OWNERS).astype(jnp.int32)
    sides = (row > 0).astype(jnp.int32) + (row < NROW - 1).astype(jnp.int32)
    return barrier, sides + 3 + (GROUP - 1) + owner * (7 + 3 * GROUP)


def gather(index, table, dest, first, count):
    def body(step, carry):
        base = pl.multiple_of(step * (STRIPS * STEP), STRIPS * STEP)
        at = first // STRIPS + step * STEP
        for q in range(STRIPS):
            for j in range(STEP):
                dest[pl.ds(base + (q * STEP + j), 1), :] = table[pl.ds(index[q][at + j], 1), :]
        return carry

    lax.fori_loop(0, count // (STRIPS * STEP), body, 0)


def widen(tile):
    return jnp.concatenate([tile, jnp.zeros((GZ, LANES - K), F32)], axis=1)


def kernel(
    counts_in, couple_in, stiffness_in, eigen, material, own_rows, send_rows,
    diag_out, off_out,
    counts, couple, stiffness, eig, halo, mat, coef, field, image, table, own_sel, own_kept, send_sel, packed, arrived, down_packed, down_arrived,
    part, sums, zsums, piece, whole, forward,
    load_sem, halo_send, halo_recv, slab_send, slab_recv, down_send, down_recv,
    one_send, one_recv, two_send, two_recv, three_send, three_recv, fwd_send, fwd_recv, index_sem, *strips,
):
    sub, row = lax.axis_index("sub"), lax.axis_index("row")
    z, place = row // GROUP, lax.rem(row, GROUP)
    barrier, greetings = start_barrier(sub, row)

    loads = [pltpu.make_async_copy(eigen.at[0], eig, load_sem.at[0])]
    own_index = [strips[o * STRIPS : (o + 1) * STRIPS] for o in (0, 1)]
    send_index = [strips[(2 + o) * STRIPS : (3 + o) * STRIPS] for o in (0, 1)]
    index_loads = []
    for kind, (rows, index) in enumerate(((own_rows, own_index), (send_rows, send_index))):
        index_loads.append([])
        for o in (1, 0):
            for q in range(STRIPS):
                index_loads[kind].append(pltpu.make_async_copy(
                    rows.at[0, o, pl.ds(q * STRIP, STRIP)], index[o][q], index_sem.at[kind, o, q]))
    for p in range(CX + 2):
        plane = jnp.clip(row * CX + (p - 1), 0, PLANES - 1)
        loads.append(pltpu.make_async_copy(material.at[0, plane], mat.at[p], load_sem.at[1 + p]))
    loads.append(pltpu.make_async_copy(counts_in, counts, load_sem.at[3 + CX]))
    loads.append(pltpu.make_async_copy(couple_in, couple, load_sem.at[4 + CX]))
    loads.append(pltpu.make_async_copy(stiffness_in, stiffness, load_sem.at[5 + CX]))
    for load in loads + index_loads[0] + index_loads[1]:
        load.start()
    loads[3 + CX].wait()
    count = counts[0]

    def kept(k):
        return (k < count).astype(F32)

    @pl.when(row == 0)
    def _():
        halo[0] = jnp.zeros((K, C, GY, GZ), BF16)

    @pl.when(row == NROW - 1)
    def _():
        halo[1] = jnp.zeros((K, C, GY, GZ), BF16)

    loads[0].wait()

    def mask_column(k, carry):
        keep = kept(k)
        for c in range(C):
            for p in range(CX):
                base = pl.multiple_of(k * (C * CX * GY) + (c * CX + p) * GY, GY)
                field[pl.ds(base, GY), :] = eig[k, c, p].astype(F32) * keep
        return carry

    lax.fori_loop(0, K, mask_column, 0)

    def across(source, at):
        return source[pl.ds(at, K, stride=C * CX * GY), :]

    def fill_table(block, carry):
        for y in range(GY):
            at = block * GY + y
            table[pl.ds(pl.multiple_of(at * GZ, GZ), GZ), :] = widen(across(field, at).T)
        return carry

    lax.fori_loop(0, C * CX, fill_table, 0)

    pl.semaphore_wait(barrier, greetings)
    up = pltpu.make_async_remote_copy(
        src_ref=eigen.at[0, :, :, CX - 1], dst_ref=halo.at[0], send_sem=halo_send.at[0],
        recv_sem=halo_recv.at[0], device_id=(sub, jnp.minimum(row + 1, NROW - 1)), device_id_type=MESH)
    down = pltpu.make_async_remote_copy(
        src_ref=eigen.at[0, :, :, 0], dst_ref=halo.at[1], send_sem=halo_send.at[1],
        recv_sem=halo_recv.at[1], device_id=(sub, jnp.maximum(row - 1, 0)), device_id_type=MESH)

    @pl.when(row < NROW - 1)
    def _():
        up.start()

    @pl.when(row > 0)
    def _():
        down.start()

    for load in index_loads[0]:
        load.wait()
    loads[4 + CX].wait()
    lane = lax.broadcasted_iota(jnp.int32, (K, LANES), 1)
    line = lax.broadcasted_iota(jnp.int32, (K, LANES), 0)
    turn = [
        jnp.where(lane == line, couple[0, o].astype(F32), F32(0)).astype(BF16) for o in (0, 1)]
    plain = jnp.where(lane == line, F32(1), F32(0)).astype(BF16)

    def turned(by, rows):
        return jnp.concatenate([
            lax.dot_general(by, rows[base : base + 256].astype(BF16), (((1,), (1,)), ((), ())),
                            preferred_element_type=F32).astype(BF16)
            for base in range(0, CHUNK, 256)], axis=1)

    slabs = []
    for e, (o, n) in enumerate(UP):
        gather(own_index[o], table, own_sel.at[e % 2], n * CHUNK, CHUNK)
        packed[e] = turned(turn[o], own_sel[e % 2])
        slab = pltpu.make_async_remote_copy(
            src_ref=packed.at[e], dst_ref=arrived.at[e],
            send_sem=slab_send.at[e], recv_sem=slab_recv.at[e],
            device_id=(at_sub(sub, o + 1), row), device_id_type=MESH)
        slab.start()
        slabs.append(slab)
    for e, (o, n) in enumerate(DOWN):
        gather(own_index[o], table, own_kept.at[e], n * CHUNK, CHUNK)

    for p in range(CX + 2):
        loads[1 + p].wait()
    loads[5 + CX].wait()
    kappa = []
    for p in range(CX + 2):
        level = mat[p]
        found = jnp.zeros((GY, GZ), F32)
        for m in range(NLEVEL):
            found = found + jnp.where(level == m, stiffness[m], F32(0))
        kappa.append(found)
    faces = []
    for p in range(CX + 1):
        face = 0.5 * (kappa[p] + kappa[p + 1])
        if p == 0:
            face = face * (row > 0).astype(F32)
        if p == CX:
            face = face * (row < NROW - 1).astype(F32)
        coef[p] = face
        faces.append(face)
    in_y = lax.broadcasted_iota(jnp.int32, (GY, GZ), 0) < GY - 1
    in_z = lax.broadcasted_iota(jnp.int32, (GY, GZ), 1) < GZ - 1
    for p in range(CX):
        mid = kappa[p + 1]
        y_up = jnp.where(in_y, 0.5 * (mid + pltpu.roll(mid, GY - 1, 0)), 0.0)
        z_up = jnp.where(in_z, 0.5 * (mid + pltpu.roll(mid, GZ - 1, 1)), 0.0)
        y_down, z_down = pltpu.roll(y_up, 1, 0), pltpu.roll(z_up, 1, 1)
        for n, face in enumerate((y_down, y_up, z_down, z_up)):
            coef[CX + 1 + 4 * p + n] = face
        along = (faces[p] + faces[p + 1], y_down + y_up, z_down + z_up)
        for c in range(C):
            coef[5 * CX + 1 + C * p + c] = along[0] + along[1] + along[2] + 2.0 * along[c]

    @pl.when(row > 0)
    def _():
        up.wait_recv()

    @pl.when(row < NROW - 1)
    def _():
        down.wait_recv()

    def apply_column(k):
        keep = kept(k)
        for c in range(C):
            def at(p):
                return pl.multiple_of(k * (C * CX * GY) + (c * CX + p) * GY, GY)

            cells = [halo[0, k, c].astype(F32) * keep]
            cells += [field[pl.ds(at(p), GY), :] for p in range(CX)]
            cells.append(halo[1, k, c].astype(F32) * keep)
            for p in range(CX):
                u = cells[p + 1]
                face = [coef[CX + 1 + 4 * p + n] for n in range(4)]
                near = [
                    coef[p] * cells[p] + coef[p + 1] * cells[p + 2],
                    face[0] * pltpu.roll(u, 1, 0) + face[1] * pltpu.roll(u, GY - 1, 0),
                    face[2] * pltpu.roll(u, 1, 1) + face[3] * pltpu.roll(u, GZ - 1, 1),
                ]
                own = coef[5 * CX + 1 + C * p + c]
                image[pl.ds(at(p), GY), :] = own * u - (near[0] + near[1] + near[2] + 2.0 * near[c])

    def apply_columns(block, carry):
        for u in range(4):
            apply_column(4 * block + u)
        return carry

    lax.fori_loop(0, K // 4, apply_columns, 0)

    def image_table(block, total):
        basis, turned = [], []
        for y in range(GY):
            at = block * GY + y
            wide = widen(across(image, at).T)
            table[pl.ds(pl.multiple_of(at * GZ, GZ), GZ), :] = wide
            turned.append(wide.astype(BF16))
            basis.append(across(field, at).astype(BF16))
        return total + jnp.dot(
            jnp.concatenate(basis, axis=1), jnp.concatenate(turned, axis=0), preferred_element_type=F32)

    diag = lax.fori_loop(0, C * CX, image_table, jnp.zeros((K, LANES), F32))

    for load in index_loads[1]:
        load.wait()
    downs = []
    for e, (o, n) in enumerate(DOWN):
        gather(send_index[o], table, own_sel.at[e % 2], n * CHUNK, CHUNK)
        down_packed[e] = turned(plain, own_sel[e % 2])
        slab = pltpu.make_async_remote_copy(
            src_ref=down_packed.at[e], dst_ref=down_arrived.at[e],
            send_sem=down_send.at[e], recv_sem=down_recv.at[e],
            device_id=(at_sub(sub, -o - 1), row), device_id_type=MESH)
        slab.start()
        downs.append(slab)
    pairs = [jnp.zeros((K, LANES), F32) for o in (0, 1)]
    for e, (o, n) in enumerate(UP):
        gather(send_index[o], table, send_sel.at[e % 2], n * CHUNK, CHUNK)
        slabs[e].wait_recv()
        pairs[o] = pairs[o] + jnp.dot(
            arrived[e], send_sel[e % 2].astype(BF16), preferred_element_type=F32)
    below = jnp.zeros((K, LANES), F32)
    for e, (o, n) in enumerate(DOWN):
        downs[e].wait_recv()
        below = below + jnp.dot(
            down_arrived[e], own_kept[e].astype(BF16), preferred_element_type=F32)
    mats = [diag, pairs[0], pairs[1], below * couple[0, 1].astype(F32)]
    for q in range(OWNERS):
        for m in range(4):
            part[q, pl.ds(8 * m, 8), :] = mats[m][8 * q : 8 * q + 8]

    is_owner = place < OWNERS
    own_q = jnp.minimum(place, OWNERS - 1)

    def landed(ref, sem):
        pltpu.make_async_copy(ref, ref, sem).wait()

    firsts = []
    for step in FAR_FIRST:
        to = lax.rem(place + step, GROUP)
        to_q = jnp.minimum(to, OWNERS - 1)
        firsts.append((to, pltpu.make_async_remote_copy(
            src_ref=part.at[to_q], dst_ref=sums.at[place],
            send_sem=one_send.at[step], recv_sem=one_recv,
            device_id=(sub, z * GROUP + to), device_id_type=MESH)))
    for to, copy in firsts:
        @pl.when(to < OWNERS)
        def _(copy=copy):
            copy.start()

    seconds = []
    for step in FAR_FIRST:
        seconds.append(pltpu.make_async_remote_copy(
            src_ref=piece.at[0], dst_ref=zsums.at[z],
            send_sem=two_send.at[step], recv_sem=two_recv,
            device_id=(sub, lax.rem(z + step, 8) * GROUP + place), device_id_type=MESH))

    thirds = []
    for o, by in ((1, -2), (2, 2), (0, -1)):
        for to in range(GROUP):
            thirds.append(pltpu.make_async_remote_copy(
                src_ref=piece.at[1, pl.ds(8 + 8 * o, 8)], dst_ref=forward.at[o, own_q],
                send_sem=fwd_send.at[o, to], recv_sem=fwd_recv,
                device_id=(at_sub(sub, by), z * GROUP + to), device_id_type=MESH))
    for step in FAR_FIRST:
        thirds.append(pltpu.make_async_remote_copy(
            src_ref=piece.at[1], dst_ref=whole.at[own_q],
            send_sem=three_send.at[step], recv_sem=three_recv,
            device_id=(sub, z * GROUP + lax.rem(place + step, GROUP)), device_id_type=MESH))

    @pl.when(is_owner)
    def _():
        sums[place] = part[own_q]
        landed(sums.at[pl.ds(0, GROUP - 1)], one_recv)
        total = sums[0]
        for q in range(1, GROUP):
            total = total + sums[q]
        piece[0] = total
        for copy in seconds:
            copy.start()
        zsums[z] = total
        landed(zsums.at[pl.ds(0, 7)], two_recv)
        total = zsums[0]
        for q in range(1, 8):
            total = total + zsums[q]
        piece[1] = total
        for copy in thirds:
            copy.start()
        whole[own_q] = total
        landed(whole.at[pl.ds(0, OWNERS - 1)], three_recv)

    @pl.when(place >= OWNERS)
    def _():
        landed(whole, three_recv)

    landed(forward, fwd_recv)

    scale = 1.0 / math.sqrt(NROW * SLAB)
    diag_out[0] = jnp.concatenate([whole[q, 0:8, :K] for q in range(OWNERS)], axis=0) * (1.0 / (C * PLANES * GY * GZ))
    def joined(ref, at):
        return jnp.concatenate([ref[q, at : at + 8, :] for q in range(OWNERS)], axis=0)

    from_above = [jnp.concatenate([forward[o, q] for q in range(OWNERS)], axis=0) for o in range(3)]
    off_out[0, 0] = (joined(whole, 16).T[:K, :] + from_above[2][:, :K]) * scale
    off_out[0, 1] = joined(whole, 8).T[:K, :] * scale
    off_out[0, 2] = from_above[0][:, :K] * scale
    off_out[0, 3] = (from_above[1][:, :K] + joined(whole, 24).T[:K, :]) * scale

    @pl.when(row < NROW - 1)
    def _():
        up.wait_send()

    @pl.when(row > 0)
    def _():
        down.wait_send()

    for slab in slabs + downs:
        slab.wait_send()
    for to, copy in firsts:
        @pl.when(to < OWNERS)
        def _(copy=copy):
            copy.wait_send()

    @pl.when(is_owner)
    def _():
        for copy in seconds + thirds:
            copy.wait_send()


def shards(eigen_basis, material, counts, couple, own_rows, send_rows, stiffness):
    hbm = pl.BlockSpec(memory_space=pltpu.HBM)
    vmem = pl.BlockSpec(memory_space=pltpu.VMEM)
    dma = pltpu.SemaphoreType.DMA
    return pl.pallas_call(
        kernel,
        out_shape=(jax.ShapeDtypeStruct((1, K, K), F32), jax.ShapeDtypeStruct((1, 4, K, K), F32)),
        in_specs=[hbm] * 7,
        out_specs=(vmem, vmem),
        scratch_shapes=[
            pltpu.SMEM((1,), jnp.int32),
            pltpu.SMEM((1, 2), jnp.int32),
            pltpu.SMEM((NLEVEL,), F32),
            pltpu.VMEM((K, C, CX, GY, GZ), BF16),
            pltpu.VMEM((2, K, C, GY, GZ), BF16),
            pltpu.VMEM((CX + 2, GY, GZ), jnp.int32),
            pltpu.VMEM((5 * CX + 1 + C * CX, GY, GZ), F32),
            pltpu.VMEM((K * C * CX * GY, GZ), F32),
            pltpu.VMEM((K * C * CX * GY, GZ), F32),
            pltpu.VMEM((ROWS, LANES), F32),
            pltpu.VMEM((2, CHUNK, LANES), F32),
            pltpu.VMEM((BACK, CHUNK, LANES), F32),
            pltpu.VMEM((2, CHUNK, LANES), F32),
            pltpu.VMEM((len(UP), K, CHUNK), BF16),
            pltpu.VMEM((len(UP), K, CHUNK), BF16),
            pltpu.VMEM((BACK, K, CHUNK), BF16),
            pltpu.VMEM((BACK, K, CHUNK), BF16),
            pltpu.VMEM((OWNERS, 32, LANES), F32),
            pltpu.VMEM((GROUP, 32, LANES), F32),
            pltpu.VMEM((8, 32, LANES), F32),
            pltpu.VMEM((2, 32, LANES), F32),
            pltpu.VMEM((OWNERS, 32, LANES), F32),
            pltpu.VMEM((3, OWNERS, 8, LANES), F32),
            dma((6 + CX,)), dma((2,)), dma((2,)), dma((len(UP),)), dma((len(UP),)), dma((BACK,)), dma((BACK,)),
            dma((GROUP,)), dma, dma((8,)), dma, dma((GROUP,)), dma, dma((3, GROUP)), dma,
            dma((2, 2, STRIPS)),
        ] + [pltpu.SMEM((STRIP,), jnp.int32) for _ in range(4 * STRIPS)],
        compiler_params=pltpu.CompilerParams(
            collective_id=0, has_side_effects=True, vmem_limit_bytes=60 * 2**20),
        name="coarse",
    )(counts, couple, stiffness, eigen_basis, material, own_rows, send_rows)


def solution(mesh):
    in_specs = (
        P("sub", None, None, "row", None, None),
        P("sub", None, None, None),
        P("sub"),
        P("sub", None),
        P("sub", None, "row"),
        P("sub", None, "row"),
        P(),
    )
    out_specs = (P("sub", None, None), P("sub", None, None, None))
    return jax.shard_map(shards, mesh=mesh, in_specs=in_specs, out_specs=out_specs, check_vma=False)
```

```python
import functools
import math

import jax
import jax.numpy as jnp
from jax import lax
from jax.experimental import pallas as pl
from jax.experimental.pallas import tpu as pltpu
from jax.sharding import PartitionSpec as P

MESH = pl.DeviceIdType.MESH
F32 = jnp.float32
BF16 = jnp.bfloat16

K = 48
C = 3
CX = 2
GY = 16
GZ = 128
CELLS = CX * GY * GZ
ROWS = C * CELLS
NSUB = 8
NROW = 64
PLANES = NROW * CX
SLAB = 4096
CHUNK = 512
NCHUNK = SLAB // CHUNK
BACK = 2
UP = [(1, n) for n in range(NCHUNK - BACK)] + [(0, n) for n in range(NCHUNK)]
DOWN = [(1, n) for n in range(NCHUNK - BACK, NCHUNK)]
FAR_FIRST = (4, 3, 5, 2, 6, 1, 7)
NLEVEL = 16
GROUP = 8
OWNERS = 6
LANES = 128
HALF = 64
STRIPS = 8
STEP = 8
STRIP = SLAB // STRIPS
PARTS = 2


def at_sub(sub, by):
    return lax.rem(sub + (by + NSUB), NSUB)


def start_barrier(sub, row):
    z, place = row // GROUP, lax.rem(row, GROUP)
    barrier = pltpu.get_barrier_semaphore()

    def signal(to_sub, to_row):
        pl.semaphore_signal(barrier, inc=1, device_id=(to_sub, to_row), device_id_type=MESH)

    @pl.when(row > 0)
    def _():
        signal(sub, row - 1)

    @pl.when(row < NROW - 1)
    def _():
        signal(sub, row + 1)

    for by in (-1, -2, 2):
        signal(at_sub(sub, by), row)
    for step in FAR_FIRST:
        signal(sub, z * GROUP + lax.rem(place + step, GROUP))

    @pl.when(place < OWNERS)
    def _():
        for step in FAR_FIRST:
            signal(sub, lax.rem(z + step, 8) * GROUP + place)

    for by in (2, -2, 1):
        for q in range(OWNERS):
            signal(at_sub(sub, by), z * GROUP + q)

    owner = (place < OWNERS).astype(jnp.int32)
    sides = (row > 0).astype(jnp.int32) + (row < NROW - 1).astype(jnp.int32)
    return barrier, sides + 3 + (GROUP - 1) + owner * (7 + 3 * GROUP)


def gather(index, table, dest, first):
    def body(step, carry):
        for part in range(PARTS):
            start = pl.multiple_of((step * PARTS + part) * (STRIPS * STEP), STRIPS * STEP)
            at = first // STRIPS + (step * PARTS + part) * STEP
            for q in range(STRIPS):
                for j in range(STEP):
                    dest[pl.ds(start + (q * STEP + j), 1), :] = table[pl.ds(index[q][at + j], 1), :]
        return carry

    lax.fori_loop(0, CHUNK // (PARTS * STRIPS * STEP), body, 0)


def widen(tile):
    return jnp.concatenate([tile, jnp.zeros((GZ, LANES - K), F32)], axis=1)


def kernel(
    counts_in, couple_in, stiffness_in, eigen, material, own_rows, send_rows,
    whole_out, forward_out,
    counts, couple, stiffness, eig, halo, mat, coef, field, image, table, own_sel, own_kept, send_sel, packed, arrived, down_packed, down_arrived,
    part, sums, zsums, piece, whole, forward,
    load_sem, halo_send, halo_recv, slab_send, slab_recv, down_send, down_recv,
    one_send, one_recv, two_send, two_recv, three_send, three_recv, fwd_send, fwd_recv, index_sem, *strips,
):
    sub, row = lax.axis_index("sub"), lax.axis_index("row")
    z, place = row // GROUP, lax.rem(row, GROUP)
    barrier, greetings = start_barrier(sub, row)

    loads = [pltpu.make_async_copy(eigen.at[0], eig, load_sem.at[0])]
    own_index = [strips[o * STRIPS : (o + 1) * STRIPS] for o in (0, 1)]
    send_index = [strips[(2 + o) * STRIPS : (3 + o) * STRIPS] for o in (0, 1)]
    index_loads = []
    for kind, (rows, index) in enumerate(((own_rows, own_index), (send_rows, send_index))):
        index_loads.append([])
        for o in (1, 0):
            for q in range(STRIPS):
                index_loads[kind].append(pltpu.make_async_copy(
                    rows.at[0, o, pl.ds(q * STRIP, STRIP)], index[o][q], index_sem.at[kind, o, q]))
    for p in range(CX + 2):
        plane = jnp.clip(row * CX + (p - 1), 0, PLANES - 1)
        loads.append(pltpu.make_async_copy(material.at[0, plane], mat.at[p], load_sem.at[1 + p]))
    loads.append(pltpu.make_async_copy(counts_in, counts, load_sem.at[3 + CX]))
    loads.append(pltpu.make_async_copy(couple_in, couple, load_sem.at[4 + CX]))
    loads.append(pltpu.make_async_copy(stiffness_in, stiffness, load_sem.at[5 + CX]))
    for load in loads + index_loads[0] + index_loads[1]:
        load.start()
    loads[3 + CX].wait()
    count = counts[0]

    def kept(k):
        return (k < count).astype(F32)

    @pl.when(row == 0)
    def _():
        halo[0] = jnp.zeros((K, C, GY, GZ), BF16)

    @pl.when(row == NROW - 1)
    def _():
        halo[1] = jnp.zeros((K, C, GY, GZ), BF16)

    loads[0].wait()

    def mask_column(k, carry):
        keep = kept(k)
        for c in range(C):
            for p in range(CX):
                base = pl.multiple_of(k * (C * CX * GY) + (c * CX + p) * GY, GY)
                field[pl.ds(base, GY), :] = eig[k, c, p].astype(F32) * keep
        return carry

    lax.fori_loop(0, K, mask_column, 0)

    def across(source, at):
        return source[pl.ds(at, K, stride=C * CX * GY), :]

    def fill_table(block, carry):
        for y in range(GY):
            at = block * GY + y
            table[pl.ds(pl.multiple_of(at * GZ, GZ), GZ), :] = widen(across(field, at).T)
        return carry

    lax.fori_loop(0, C * CX, fill_table, 0)

    pl.semaphore_wait(barrier, greetings)
    up = pltpu.make_async_remote_copy(
        src_ref=eigen.at[0, :, :, CX - 1], dst_ref=halo.at[0], send_sem=halo_send.at[0],
        recv_sem=halo_recv.at[0], device_id=(sub, jnp.minimum(row + 1, NROW - 1)), device_id_type=MESH)
    down = pltpu.make_async_remote_copy(
        src_ref=eigen.at[0, :, :, 0], dst_ref=halo.at[1], send_sem=halo_send.at[1],
        recv_sem=halo_recv.at[1], device_id=(sub, jnp.maximum(row - 1, 0)), device_id_type=MESH)

    @pl.when(row < NROW - 1)
    def _():
        up.start()

    @pl.when(row > 0)
    def _():
        down.start()

    for load in index_loads[0]:
        load.wait()
    loads[4 + CX].wait()
    lane = lax.broadcasted_iota(jnp.int32, (K, LANES), 1)
    line = lax.broadcasted_iota(jnp.int32, (K, LANES), 0)
    turn = [
        jnp.where(lane == line, couple[0, o].astype(F32), F32(0)).astype(BF16) for o in (0, 1)]
    plain = jnp.where(lane == line, F32(1), F32(0)).astype(BF16)

    def turned(by, rows):
        return jnp.concatenate([
            lax.dot_general(by, rows[base : base + 256].astype(BF16), (((1,), (1,)), ((), ())),
                            preferred_element_type=F32).astype(BF16)
            for base in range(0, CHUNK, 256)], axis=1)

    slabs = []
    for e, (o, n) in enumerate(UP):
        gather(own_index[o], table, own_sel.at[e % 2], n * CHUNK)
        packed[e] = turned(turn[o], own_sel[e % 2])
        slab = pltpu.make_async_remote_copy(
            src_ref=packed.at[e], dst_ref=arrived.at[e],
            send_sem=slab_send.at[e], recv_sem=slab_recv.at[e],
            device_id=(at_sub(sub, o + 1), row), device_id_type=MESH)
        slab.start()
        slabs.append(slab)
    for e, (o, n) in enumerate(DOWN):
        gather(own_index[o], table, own_kept.at[e], n * CHUNK)

    for p in range(CX + 2):
        loads[1 + p].wait()
    loads[5 + CX].wait()
    kappa = []
    for p in range(CX + 2):
        level = mat[p]
        found = jnp.zeros((GY, GZ), F32)
        for m in range(NLEVEL):
            found = found + jnp.where(level == m, stiffness[m], F32(0))
        kappa.append(found)
    faces = []
    for p in range(CX + 1):
        face = 0.5 * (kappa[p] + kappa[p + 1])
        if p == 0:
            face = face * (row > 0).astype(F32)
        if p == CX:
            face = face * (row < NROW - 1).astype(F32)
        coef[p] = face
        faces.append(face)
    in_y = lax.broadcasted_iota(jnp.int32, (GY, GZ), 0) < GY - 1
    in_z = lax.broadcasted_iota(jnp.int32, (GY, GZ), 1) < GZ - 1
    for p in range(CX):
        mid = kappa[p + 1]
        y_up = jnp.where(in_y, 0.5 * (mid + pltpu.roll(mid, GY - 1, 0)), 0.0)
        z_up = jnp.where(in_z, 0.5 * (mid + pltpu.roll(mid, GZ - 1, 1)), 0.0)
        y_down, z_down = pltpu.roll(y_up, 1, 0), pltpu.roll(z_up, 1, 1)
        for n, face in enumerate((y_down, y_up, z_down, z_up)):
            coef[CX + 1 + 4 * p + n] = face
        along = (faces[p] + faces[p + 1], y_down + y_up, z_down + z_up)
        for c in range(C):
            coef[5 * CX + 1 + C * p + c] = along[0] + along[1] + along[2] + 2.0 * along[c]

    @pl.when(row > 0)
    def _():
        up.wait_recv()

    @pl.when(row < NROW - 1)
    def _():
        down.wait_recv()

    def apply_column(k):
        keep = kept(k)
        for c in range(C):
            def at(p):
                return pl.multiple_of(k * (C * CX * GY) + (c * CX + p) * GY, GY)

            cells = [halo[0, k, c].astype(F32) * keep]
            cells += [field[pl.ds(at(p), GY), :] for p in range(CX)]
            cells.append(halo[1, k, c].astype(F32) * keep)
            for p in range(CX):
                u = cells[p + 1]
                face = [coef[CX + 1 + 4 * p + n] for n in range(4)]
                near = [
                    coef[p] * cells[p] + coef[p + 1] * cells[p + 2],
                    face[0] * pltpu.roll(u, 1, 0) + face[1] * pltpu.roll(u, GY - 1, 0),
                    face[2] * pltpu.roll(u, 1, 1) + face[3] * pltpu.roll(u, GZ - 1, 1),
                ]
                own = coef[5 * CX + 1 + C * p + c]
                image[pl.ds(at(p), GY), :] = own * u - (near[0] + near[1] + near[2] + 2.0 * near[c])

    def apply_columns(block, carry):
        for u in range(4):
            apply_column(4 * block + u)
        return carry

    lax.fori_loop(0, K // 4, apply_columns, 0)

    def image_table(block, total):
        basis, turned = [], []
        for y in range(GY):
            at = block * GY + y
            wide = widen(across(image, at).T)
            table[pl.ds(pl.multiple_of(at * GZ, GZ), GZ), :] = wide
            turned.append(wide.astype(BF16))
            basis.append(across(field, at).astype(BF16))
        return total + jnp.dot(
            jnp.concatenate(basis, axis=1), jnp.concatenate(turned, axis=0), preferred_element_type=F32)

    diag = lax.fori_loop(0, C * CX, image_table, jnp.zeros((K, LANES), F32))

    for load in index_loads[1]:
        load.wait()
    downs = []
    for e, (o, n) in enumerate(DOWN):
        gather(send_index[o], table, own_sel.at[e % 2], n * CHUNK)
        down_packed[e] = turned(plain, own_sel[e % 2])
        slab = pltpu.make_async_remote_copy(
            src_ref=down_packed.at[e], dst_ref=down_arrived.at[e],
            send_sem=down_send.at[e], recv_sem=down_recv.at[e],
            device_id=(at_sub(sub, -o - 1), row), device_id_type=MESH)
        slab.start()
        downs.append(slab)
    pairs = [jnp.zeros((K, LANES), F32) for o in (0, 1)]
    for e, (o, n) in enumerate(UP):
        gather(send_index[o], table, send_sel.at[e % 2], n * CHUNK)
        slabs[e].wait_recv()
        pairs[o] = pairs[o] + jnp.dot(
            arrived[e], send_sel[e % 2].astype(BF16), preferred_element_type=F32)
    below = jnp.zeros((K, LANES), F32)
    for e in range(BACK):
        downs[e].wait_recv()
        below = below + jnp.dot(
            down_arrived[e], own_kept[e].astype(BF16), preferred_element_type=F32)
    below = below * couple[0, 1].astype(F32)
    mats = [diag + pltpu.roll(pairs[0], HALF, 1), pairs[1] + pltpu.roll(below, HALF, 1)]
    for q in range(OWNERS):
        for m in range(2):
            part[q, pl.ds(8 * m, 8), :] = mats[m][8 * q : 8 * q + 8]

    is_owner = place < OWNERS
    own_q = jnp.minimum(place, OWNERS - 1)

    def landed(ref, sem):
        pltpu.make_async_copy(ref, ref, sem).wait()

    firsts = []
    for step in FAR_FIRST:
        to = lax.rem(place + step, GROUP)
        to_q = jnp.minimum(to, OWNERS - 1)
        firsts.append((to, pltpu.make_async_remote_copy(
            src_ref=part.at[to_q], dst_ref=sums.at[place],
            send_sem=one_send.at[step], recv_sem=one_recv,
            device_id=(sub, z * GROUP + to), device_id_type=MESH)))
    for to, copy in firsts:
        @pl.when(to < OWNERS)
        def _(copy=copy):
            copy.start()

    seconds = []
    for step in FAR_FIRST:
        seconds.append(pltpu.make_async_remote_copy(
            src_ref=piece.at[0], dst_ref=zsums.at[z],
            send_sem=two_send, recv_sem=two_recv,
            device_id=(sub, lax.rem(z + step, 8) * GROUP + place), device_id_type=MESH))

    thirds = []
    for o, by in ((1, -2), (2, 2), (0, -1)):
        for to in range(GROUP):
            thirds.append(pltpu.make_async_remote_copy(
                src_ref=piece.at[1, pl.ds(8 if o else 0, 8)], dst_ref=forward.at[o, own_q],
                send_sem=fwd_send.at[o], recv_sem=fwd_recv,
                device_id=(at_sub(sub, by), z * GROUP + to), device_id_type=MESH))
    for step in FAR_FIRST:
        thirds.append(pltpu.make_async_remote_copy(
            src_ref=piece.at[1], dst_ref=whole.at[own_q],
            send_sem=three_send, recv_sem=three_recv,
            device_id=(sub, z * GROUP + lax.rem(place + step, GROUP)), device_id_type=MESH))

    @pl.when(row < NROW - 1)
    def _():
        up.wait_send()

    @pl.when(row > 0)
    def _():
        down.wait_send()

    for slab in slabs + downs:
        slab.wait_send()

    @pl.when(is_owner)
    def _():
        sums[place] = part[own_q]
        landed(sums.at[pl.ds(0, GROUP - 1)], one_recv)
        total = sums[0]
        for q in range(1, GROUP):
            total = total + sums[q]
        piece[0] = total
        for copy in seconds:
            copy.start()
        zsums[z] = total
        landed(zsums.at[pl.ds(0, 7)], two_recv)
        total = zsums[0]
        for q in range(1, 8):
            total = total + zsums[q]
        piece[1] = total
        for copy in thirds:
            copy.start()
        whole[own_q] = total
        landed(zsums.at[pl.ds(0, 7)], two_send)
        landed(whole.at[pl.ds(0, OWNERS - 1)], three_recv)

    for to, copy in firsts:
        @pl.when(to < OWNERS)
        def _(copy=copy):
            copy.wait_send()

    @pl.when(place >= OWNERS)
    def _():
        landed(whole, three_recv)

    landed(forward, fwd_recv)

    whole_out[...] = whole[...]
    forward_out[...] = forward[...]

    @pl.when(is_owner)
    def _():
        for o in range(3):
            landed(sums.at[pl.ds(0, GROUP // 2)], fwd_send.at[o])
        landed(sums.at[pl.ds(0, GROUP - 1)], three_send)


def assemble(whole, forward, diag_out, off_out):
    scale = 1.0 / math.sqrt(NROW * SLAB)
    diag_pair, pair_below = [
        jnp.concatenate([whole[q, at : at + 8] for q in range(OWNERS)], axis=0) for at in (0, 8)]
    from_above = [jnp.concatenate([forward[o, q] for q in range(OWNERS)], axis=0) for o in range(3)]
    diag_out[0] = diag_pair[:, :K] * (1.0 / (C * PLANES * GY * GZ))
    off_out[0, 0] = (pair_below.T[:K] + pltpu.roll(from_above[2], HALF, 1)[:, :K]) * scale
    off_out[0, 1] = diag_pair.T[HALF : HALF + K] * scale
    off_out[0, 2] = pltpu.roll(from_above[0], HALF, 1)[:, :K] * scale
    off_out[0, 3] = (from_above[1][:, :K] + pair_below.T[HALF : HALF + K]) * scale


def shards(eigen_basis, material, counts, couple, own_rows, send_rows, stiffness):
    hbm = pl.BlockSpec(memory_space=pltpu.HBM)
    vmem = pl.BlockSpec(memory_space=pltpu.VMEM)
    dma = pltpu.SemaphoreType.DMA
    sums = pl.pallas_call(
        kernel,
        out_shape=(
            jax.ShapeDtypeStruct((OWNERS, 16, LANES), F32),
            jax.ShapeDtypeStruct((3, OWNERS, 8, LANES), F32),
        ),
        in_specs=[hbm] * 7,
        out_specs=(vmem, vmem),
        scratch_shapes=[
            pltpu.SMEM((1,), jnp.int32),
            pltpu.SMEM((1, 2), jnp.int32),
            pltpu.SMEM((NLEVEL,), F32),
            pltpu.VMEM((K, C, CX, GY, GZ), BF16),
            pltpu.VMEM((2, K, C, GY, GZ), BF16),
            pltpu.VMEM((CX + 2, GY, GZ), jnp.int32),
            pltpu.VMEM((5 * CX + 1 + C * CX, GY, GZ), F32),
            pltpu.VMEM((K * C * CX * GY, GZ), F32),
            pltpu.VMEM((K * C * CX * GY, GZ), F32),
            pltpu.VMEM((ROWS, LANES), F32),
            pltpu.VMEM((2, CHUNK, LANES), F32),
            pltpu.VMEM((BACK, CHUNK, LANES), F32),
            pltpu.VMEM((2, CHUNK, LANES), F32),
            pltpu.VMEM((len(UP), K, CHUNK), BF16),
            pltpu.VMEM((len(UP), K, CHUNK), BF16),
            pltpu.VMEM((BACK, K, CHUNK), BF16),
            pltpu.VMEM((BACK, K, CHUNK), BF16),
            pltpu.VMEM((OWNERS, 16, LANES), F32),
            pltpu.VMEM((GROUP, 16, LANES), F32),
            pltpu.VMEM((8, 16, LANES), F32),
            pltpu.VMEM((2, 16, LANES), F32),
            pltpu.VMEM((OWNERS, 16, LANES), F32),
            pltpu.VMEM((3, OWNERS, 8, LANES), F32),
            dma((6 + CX,)), dma((2,)), dma((2,)), dma((len(UP),)), dma((len(UP),)), dma((BACK,)), dma((BACK,)),
            dma((GROUP,)), dma, dma, dma, dma, dma, dma((3,)), dma,
            dma((2, 2, STRIPS)),
        ] + [pltpu.SMEM((STRIP,), jnp.int32) for _ in range(4 * STRIPS)],
        compiler_params=pltpu.CompilerParams(
            collective_id=0, has_side_effects=True, vmem_limit_bytes=60 * 2**20),
        name="coarse",
    )(counts, couple, stiffness, eigen_basis, material, own_rows, send_rows)
    return pl.pallas_call(
        assemble,
        out_shape=(jax.ShapeDtypeStruct((1, K, K), F32), jax.ShapeDtypeStruct((1, 4, K, K), F32)),
        in_specs=[vmem, vmem],
        out_specs=(vmem, vmem),
        name="assemble",
    )(*sums)


def solution(mesh):
    in_specs = (
        P("sub", None, None, "row", None, None),
        P("sub", None, None, None),
        P("sub"),
        P("sub", None),
        P("sub", None, "row"),
        P("sub", None, "row"),
        P(),
    )
    out_specs = (P("sub", None, None), P("sub", None, None, None))
    return jax.shard_map(shards, mesh=mesh, in_specs=in_specs, out_specs=out_specs, check_vma=False)
```

```python
import functools
import math

import jax
import jax.numpy as jnp
from jax import lax
from jax.experimental import pallas as pl
from jax.experimental.pallas import tpu as pltpu
from jax.sharding import PartitionSpec as P

MESH = pl.DeviceIdType.MESH
F32 = jnp.float32
BF16 = jnp.bfloat16

K = 48
C = 3
CX = 2
GY = 16
GZ = 128
CELLS = CX * GY * GZ
ROWS = C * CELLS
NSUB = 8
NROW = 64
PLANES = NROW * CX
SLAB = 4096
CHUNK = 512
NCHUNK = SLAB // CHUNK
BACK = 3
UP = [(1, n) for n in range(NCHUNK - BACK)] + [(0, n) for n in range(NCHUNK)]
DOWN = [(1, n) for n in range(NCHUNK - BACK, NCHUNK)]
BEFORE = 3
PIECE = 16
FAR_FIRST = (4, 3, 5, 2, 6, 1, 7)
NLEVEL = 16
GROUP = 8
OWNERS = 6
LANES = 128
HALF = 64
STRIPS = 8
STEP = 8
STRIP = SLAB // STRIPS
PARTS = 2


def at_sub(sub, by):
    return lax.rem(sub + (by + NSUB), NSUB)


def start_barrier(sub, row):
    z, place = row // GROUP, lax.rem(row, GROUP)
    barrier = pltpu.get_barrier_semaphore()

    def signal(to_sub, to_row):
        pl.semaphore_signal(barrier, inc=1, device_id=(to_sub, to_row), device_id_type=MESH)

    @pl.when(row > 0)
    def _():
        signal(sub, row - 1)

    @pl.when(row < NROW - 1)
    def _():
        signal(sub, row + 1)

    for by in (-1, -2, 2):
        signal(at_sub(sub, by), row)
    for step in FAR_FIRST:
        signal(sub, z * GROUP + lax.rem(place + step, GROUP))

    @pl.when(place < OWNERS)
    def _():
        for step in FAR_FIRST:
            signal(sub, lax.rem(z + step, 8) * GROUP + place)

    for by in (2, -2, 1):
        for q in range(OWNERS):
            signal(at_sub(sub, by), z * GROUP + q)

    owner = (place < OWNERS).astype(jnp.int32)
    sides = (row > 0).astype(jnp.int32) + (row < NROW - 1).astype(jnp.int32)
    return barrier, sides + 3 + (GROUP - 1) + owner * (7 + 3 * GROUP)


def gather(index, table, dest, first):
    def body(step, carry):
        for part in range(PARTS):
            start = pl.multiple_of((step * PARTS + part) * (STRIPS * STEP), STRIPS * STEP)
            at = first // STRIPS + (step * PARTS + part) * STEP
            for q in range(STRIPS):
                for j in range(STEP):
                    dest[pl.ds(start + (q * STEP + j), 1), :] = table[pl.ds(index[q][at + j], 1), :]
        return carry

    lax.fori_loop(0, CHUNK // (PARTS * STRIPS * STEP), body, 0)


def widen(tile):
    return jnp.concatenate([tile, jnp.zeros((GZ, LANES - K), F32)], axis=1)


def kernel(
    counts_in, couple_in, stiffness_in, eigen, material, own_rows, send_rows,
    whole_out, forward_out,
    counts, couple, stiffness, eig, halo, mat, coef, field, image, table, image_rows, own_sel, own_kept, send_sel, packed, arrived, down_packed, down_arrived,
    part, sums, zsums, piece, whole, forward,
    load_sem, halo_send, halo_recv, slab_send, slab_recv, down_send, down_recv,
    one_send, one_recv, two_send, two_recv, three_send, three_recv, fwd_send, fwd_recv, index_sem, eigen_sem, *strips,
):
    sub, row = lax.axis_index("sub"), lax.axis_index("row")
    z, place = row // GROUP, lax.rem(row, GROUP)
    loads = [None]
    own_index = [strips[o * STRIPS : (o + 1) * STRIPS] for o in (0, 1)]
    send_index = [strips[(2 + o) * STRIPS : (3 + o) * STRIPS] for o in (0, 1)]
    index_loads = []
    for kind, (rows, index) in enumerate(((own_rows, own_index), (send_rows, send_index))):
        index_loads.append([])
        for o in (1, 0):
            for q in range(STRIPS):
                index_loads[kind].append(pltpu.make_async_copy(
                    rows.at[0, o, pl.ds(q * STRIP, STRIP)], index[o][q], index_sem.at[kind, o, q]))
    for p in range(CX + 2):
        plane = jnp.clip(row * CX + (p - 1), 0, PLANES - 1)
        loads.append(pltpu.make_async_copy(material.at[0, plane], mat.at[p], load_sem.at[1 + p]))
    loads.append(pltpu.make_async_copy(counts_in, counts, load_sem.at[3 + CX]))
    loads.append(pltpu.make_async_copy(couple_in, couple, load_sem.at[4 + CX]))
    loads.append(pltpu.make_async_copy(stiffness_in, stiffness, load_sem.at[5 + CX]))
    def eigen_load(c, p):
        return pltpu.make_async_copy(eigen.at[0, :, c, p], eig.at[:, c, p], eigen_sem.at[c * CX + p])

    loads[3 + CX].start()
    for c in range(C):
        for p in range(CX):
            eigen_load(c, p).start()
    barrier, greetings = start_barrier(sub, row)
    for load in index_loads[0] + loads[1 : 3 + CX] + loads[4 + CX :] + index_loads[1]:
        load.start()
    loads[3 + CX].wait()
    count = counts[0]

    def kept(k):
        return (k < count).astype(F32)

    @pl.when(row == 0)
    def _():
        halo[0] = jnp.zeros((K, C, GY, GZ), BF16)

    @pl.when(row == NROW - 1)
    def _():
        halo[1] = jnp.zeros((K, C, GY, GZ), BF16)

    def across(source, at):
        return source[pl.ds(at, K, stride=C * CX * GY), :]

    def fill_table(block, carry):
        c, p = block // CX, lax.rem(block, CX)
        eigen_load(c, p).wait()
        for k in range(K):
            base = pl.multiple_of(k * (C * CX * GY) + block * GY, GY)
            field[pl.ds(base, GY), :] = eig[k, c, p].astype(F32) * keeps[k]
        for y in range(GY):
            at = block * GY + y
            table[pl.ds(pl.multiple_of(at * GZ, GZ), GZ), :] = widen(across(field, at).T)
        return carry

    keeps = [kept(k) for k in range(K)]
    lax.fori_loop(0, BEFORE, fill_table, 0)

    pl.semaphore_wait(barrier, greetings)
    def piece_of(h, side, to):
        some = pl.ds(h * PIECE, PIECE)
        return pltpu.make_async_remote_copy(
            src_ref=eigen.at[0, some, :, (CX - 1) * (1 - side)], dst_ref=halo.at[side, some],
            send_sem=halo_send.at[side, h], recv_sem=halo_recv.at[side, h],
            device_id=(sub, to), device_id_type=MESH)

    pieces = range(K // PIECE)
    ups = [piece_of(h, 0, jnp.minimum(row + 1, NROW - 1)) for h in pieces]
    downs_x = [piece_of(h, 1, jnp.maximum(row - 1, 0)) for h in pieces]
    for h in pieces:
        @pl.when(row < NROW - 1)
        def _(h=h):
            ups[h].start()

        @pl.when(row > 0)
        def _(h=h):
            downs_x[h].start()

    lax.fori_loop(BEFORE, C * CX, fill_table, 0)

    for load in index_loads[0]:
        load.wait()
    loads[4 + CX].wait()
    lane = lax.broadcasted_iota(jnp.int32, (K, LANES), 1)
    line = lax.broadcasted_iota(jnp.int32, (K, LANES), 0)
    turn = [
        jnp.where(lane == line, couple[0, o].astype(F32), F32(0)).astype(BF16) for o in (0, 1)]
    plain = jnp.where(lane == line, F32(1), F32(0)).astype(BF16)

    def turned(by, rows):
        return jnp.concatenate([
            lax.dot_general(by, rows[base : base + 256].astype(BF16), (((1,), (1,)), ((), ())),
                            preferred_element_type=F32).astype(BF16)
            for base in range(0, CHUNK, 256)], axis=1)

    slabs = []
    for e, (o, n) in enumerate(UP):
        gather(own_index[o], table, own_sel.at[e % 2], n * CHUNK)
        packed[e] = turned(turn[o], own_sel[e % 2])
        slab = pltpu.make_async_remote_copy(
            src_ref=packed.at[e], dst_ref=arrived.at[e],
            send_sem=slab_send.at[e], recv_sem=slab_recv.at[e],
            device_id=(at_sub(sub, o + 1), row), device_id_type=MESH)
        slab.start()
        slabs.append(slab)
    for p in range(CX + 2):
        loads[1 + p].wait()
    loads[5 + CX].wait()
    kappa = []
    for p in range(CX + 2):
        level = mat[p]
        found = jnp.zeros((GY, GZ), F32)
        for m in range(NLEVEL):
            found = found + jnp.where(level == m, stiffness[m], F32(0))
        kappa.append(found)
    faces = []
    for p in range(CX + 1):
        face = 0.5 * (kappa[p] + kappa[p + 1])
        if p == 0:
            face = face * (row > 0).astype(F32)
        if p == CX:
            face = face * (row < NROW - 1).astype(F32)
        coef[p] = face
        faces.append(face)
    in_y = lax.broadcasted_iota(jnp.int32, (GY, GZ), 0) < GY - 1
    in_z = lax.broadcasted_iota(jnp.int32, (GY, GZ), 1) < GZ - 1
    for p in range(CX):
        mid = kappa[p + 1]
        y_up = jnp.where(in_y, 0.5 * (mid + pltpu.roll(mid, GY - 1, 0)), 0.0)
        z_up = jnp.where(in_z, 0.5 * (mid + pltpu.roll(mid, GZ - 1, 1)), 0.0)
        y_down, z_down = pltpu.roll(y_up, 1, 0), pltpu.roll(z_up, 1, 1)
        for n, face in enumerate((y_down, y_up, z_down, z_up)):
            coef[CX + 1 + 4 * p + n] = face
        along = (faces[p] + faces[p + 1], y_down + y_up, z_down + z_up)
        for c in range(C):
            coef[5 * CX + 1 + C * p + c] = along[0] + along[1] + along[2] + 2.0 * along[c]

    def apply_column(k):
        keep = kept(k)
        for c in range(C):
            def at(p):
                return pl.multiple_of(k * (C * CX * GY) + (c * CX + p) * GY, GY)

            cells = [halo[0, k, c].astype(F32) * keep]
            cells += [field[pl.ds(at(p), GY), :] for p in range(CX)]
            cells.append(halo[1, k, c].astype(F32) * keep)
            for p in range(CX):
                u = cells[p + 1]
                face = [coef[CX + 1 + 4 * p + n] for n in range(4)]
                near = [
                    coef[p] * cells[p] + coef[p + 1] * cells[p + 2],
                    face[0] * pltpu.roll(u, 1, 0) + face[1] * pltpu.roll(u, GY - 1, 0),
                    face[2] * pltpu.roll(u, 1, 1) + face[3] * pltpu.roll(u, GZ - 1, 1),
                ]
                own = coef[5 * CX + 1 + C * p + c]
                image[pl.ds(at(p), GY), :] = own * u - (near[0] + near[1] + near[2] + 2.0 * near[c])

    def apply_columns(block, carry):
        for u in range(4):
            apply_column(4 * block + u)
        return carry

    for h in pieces:
        @pl.when(row > 0)
        def _(h=h):
            ups[h].wait_recv()

        @pl.when(row < NROW - 1)
        def _(h=h):
            downs_x[h].wait_recv()

        lax.fori_loop(h * PIECE // 4, (h + 1) * PIECE // 4, apply_columns, 0)

    def image_table(block, total):
        basis, turned = [], []
        for y in range(GY):
            at = block * GY + y
            wide = widen(across(image, at).T)
            image_rows[pl.ds(pl.multiple_of(at * GZ, GZ), GZ), :] = wide
            turned.append(wide.astype(BF16))
            basis.append(across(field, at).astype(BF16))
        return total + jnp.dot(
            jnp.concatenate(basis, axis=1), jnp.concatenate(turned, axis=0), preferred_element_type=F32)

    diag = lax.fori_loop(0, C * CX, image_table, jnp.zeros((K, LANES), F32))

    for load in index_loads[1]:
        load.wait()
    downs = []
    for e, (o, n) in enumerate(DOWN):
        gather(send_index[o], image_rows, own_sel.at[e % 2], n * CHUNK)
        down_packed[e] = turned(plain, own_sel[e % 2])
        slab = pltpu.make_async_remote_copy(
            src_ref=down_packed.at[e], dst_ref=down_arrived.at[e],
            send_sem=down_send.at[e], recv_sem=down_recv.at[e],
            device_id=(at_sub(sub, -o - 1), row), device_id_type=MESH)
        slab.start()
        downs.append(slab)
    for e, (o, n) in enumerate(DOWN):
        gather(own_index[o], table, own_kept.at[e], n * CHUNK)

    pairs = [jnp.zeros((K, LANES), F32) for o in (0, 1)]
    for e, (o, n) in enumerate(UP):
        gather(send_index[o], image_rows, send_sel.at[e % 2], n * CHUNK)
        slabs[e].wait_recv()
        pairs[o] = pairs[o] + jnp.dot(
            arrived[e], send_sel[e % 2].astype(BF16), preferred_element_type=F32)
    below = jnp.zeros((K, LANES), F32)
    for e in range(BACK):
        downs[e].wait_recv()
        below = below + jnp.dot(
            down_arrived[e], own_kept[e].astype(BF16), preferred_element_type=F32)
    below = below * couple[0, 1].astype(F32)
    mats = [diag + pltpu.roll(pairs[0], HALF, 1), pairs[1] + pltpu.roll(below, HALF, 1)]
    for q in range(OWNERS):
        for m in range(2):
            part[q, pl.ds(8 * m, 8), :] = mats[m][8 * q : 8 * q + 8]

    is_owner = place < OWNERS
    own_q = jnp.minimum(place, OWNERS - 1)

    def landed(ref, sem):
        pltpu.make_async_copy(ref, ref, sem).wait()

    firsts = []
    for step in FAR_FIRST:
        to = lax.rem(place + step, GROUP)
        to_q = jnp.minimum(to, OWNERS - 1)
        firsts.append((to, pltpu.make_async_remote_copy(
            src_ref=part.at[to_q], dst_ref=sums.at[place],
            send_sem=one_send.at[step], recv_sem=one_recv,
            device_id=(sub, z * GROUP + to), device_id_type=MESH)))
    for to, copy in firsts:
        @pl.when(to < OWNERS)
        def _(copy=copy):
            copy.start()

    seconds = []
    for step in FAR_FIRST:
        seconds.append(pltpu.make_async_remote_copy(
            src_ref=piece.at[0], dst_ref=zsums.at[z],
            send_sem=two_send, recv_sem=two_recv,
            device_id=(sub, lax.rem(z + step, 8) * GROUP + place), device_id_type=MESH))

    thirds = []
    for o, by in ((1, -2), (2, 2), (0, -1)):
        for to in range(GROUP):
            thirds.append(pltpu.make_async_remote_copy(
                src_ref=piece.at[1, pl.ds(8 if o else 0, 8)], dst_ref=forward.at[o, own_q],
                send_sem=fwd_send.at[o], recv_sem=fwd_recv,
                device_id=(at_sub(sub, by), z * GROUP + to), device_id_type=MESH))
    for step in FAR_FIRST:
        thirds.append(pltpu.make_async_remote_copy(
            src_ref=piece.at[1], dst_ref=whole.at[own_q],
            send_sem=three_send, recv_sem=three_recv,
            device_id=(sub, z * GROUP + lax.rem(place + step, GROUP)), device_id_type=MESH))

    for h in pieces:
        @pl.when(row < NROW - 1)
        def _(h=h):
            ups[h].wait_send()

        @pl.when(row > 0)
        def _(h=h):
            downs_x[h].wait_send()

    for slab in slabs + downs:
        slab.wait_send()

    @pl.when(is_owner)
    def _():
        sums[place] = part[own_q]
        landed(sums.at[pl.ds(0, GROUP - 1)], one_recv)
        total = sums[0]
        for q in range(1, GROUP):
            total = total + sums[q]
        piece[0] = total
        for copy in seconds:
            copy.start()
        zsums[z] = total
        landed(zsums.at[pl.ds(0, 7)], two_recv)
        total = zsums[0]
        for q in range(1, 8):
            total = total + zsums[q]
        piece[1] = total
        for copy in thirds:
            copy.start()
        whole[own_q] = total
        landed(zsums.at[pl.ds(0, 7)], two_send)
        landed(whole.at[pl.ds(0, OWNERS - 1)], three_recv)

    for to, copy in firsts:
        @pl.when(to < OWNERS)
        def _(copy=copy):
            copy.wait_send()

    @pl.when(place >= OWNERS)
    def _():
        landed(whole, three_recv)

    landed(forward, fwd_recv)

    whole_out[...] = whole[...]
    forward_out[...] = forward[...]

    @pl.when(is_owner)
    def _():
        for o in range(3):
            landed(sums.at[pl.ds(0, GROUP // 2)], fwd_send.at[o])
        landed(sums.at[pl.ds(0, GROUP - 1)], three_send)


def assemble(whole, forward, diag_out, off_out):
    scale = 1.0 / math.sqrt(NROW * SLAB)
    diag_pair, pair_below = [
        jnp.concatenate([whole[q, at : at + 8] for q in range(OWNERS)], axis=0) for at in (0, 8)]
    from_above = [jnp.concatenate([forward[o, q] for q in range(OWNERS)], axis=0) for o in range(3)]
    diag_out[0] = diag_pair[:, :K] * (1.0 / (C * PLANES * GY * GZ))
    off_out[0, 0] = (pair_below.T[:K] + pltpu.roll(from_above[2], HALF, 1)[:, :K]) * scale
    off_out[0, 1] = diag_pair.T[HALF : HALF + K] * scale
    off_out[0, 2] = pltpu.roll(from_above[0], HALF, 1)[:, :K] * scale
    off_out[0, 3] = (from_above[1][:, :K] + pair_below.T[HALF : HALF + K]) * scale


def shards(eigen_basis, material, counts, couple, own_rows, send_rows, stiffness):
    hbm = pl.BlockSpec(memory_space=pltpu.HBM)
    vmem = pl.BlockSpec(memory_space=pltpu.VMEM)
    dma = pltpu.SemaphoreType.DMA
    sums = pl.pallas_call(
        kernel,
        out_shape=(
            jax.ShapeDtypeStruct((OWNERS, 16, LANES), F32),
            jax.ShapeDtypeStruct((3, OWNERS, 8, LANES), F32),
        ),
        in_specs=[hbm] * 7,
        out_specs=(vmem, vmem),
        scratch_shapes=[
            pltpu.SMEM((1,), jnp.int32),
            pltpu.SMEM((1, 2), jnp.int32),
            pltpu.SMEM((NLEVEL,), F32),
            pltpu.VMEM((K, C, CX, GY, GZ), BF16),
            pltpu.VMEM((2, K, C, GY, GZ), BF16),
            pltpu.VMEM((CX + 2, GY, GZ), jnp.int32),
            pltpu.VMEM((5 * CX + 1 + C * CX, GY, GZ), F32),
            pltpu.VMEM((K * C * CX * GY, GZ), F32),
            pltpu.VMEM((K * C * CX * GY, GZ), F32),
            pltpu.VMEM((ROWS, LANES), F32),
            pltpu.VMEM((ROWS, LANES), F32),
            pltpu.VMEM((2, CHUNK, LANES), F32),
            pltpu.VMEM((BACK, CHUNK, LANES), F32),
            pltpu.VMEM((2, CHUNK, LANES), F32),
            pltpu.VMEM((len(UP), K, CHUNK), BF16),
            pltpu.VMEM((len(UP), K, CHUNK), BF16),
            pltpu.VMEM((BACK, K, CHUNK), BF16),
            pltpu.VMEM((BACK, K, CHUNK), BF16),
            pltpu.VMEM((OWNERS, 16, LANES), F32),
            pltpu.VMEM((GROUP, 16, LANES), F32),
            pltpu.VMEM((8, 16, LANES), F32),
            pltpu.VMEM((2, 16, LANES), F32),
            pltpu.VMEM((OWNERS, 16, LANES), F32),
            pltpu.VMEM((3, OWNERS, 8, LANES), F32),
            dma((6 + CX,)), dma((2, K // PIECE)), dma((2, K // PIECE)), dma((len(UP),)), dma((len(UP),)), dma((BACK,)), dma((BACK,)),
            dma((GROUP,)), dma, dma, dma, dma, dma, dma((3,)), dma,
            dma((2, 2, STRIPS)), dma((C * CX,)),
        ] + [pltpu.SMEM((STRIP,), jnp.int32) for _ in range(4 * STRIPS)],
        compiler_params=pltpu.CompilerParams(
            collective_id=0, has_side_effects=True, vmem_limit_bytes=60 * 2**20),
        name="coarse",
    )(counts, couple, stiffness, eigen_basis, material, own_rows, send_rows)
    return pl.pallas_call(
        assemble,
        out_shape=(jax.ShapeDtypeStruct((1, K, K), F32), jax.ShapeDtypeStruct((1, 4, K, K), F32)),
        in_specs=[vmem, vmem],
        out_specs=(vmem, vmem),
        name="assemble",
    )(*sums)


def solution(mesh):
    in_specs = (
        P("sub", None, None, "row", None, None),
        P("sub", None, None, None),
        P("sub"),
        P("sub", None),
        P("sub", None, "row"),
        P("sub", None, "row"),
        P(),
    )
    out_specs = (P("sub", None, None), P("sub", None, None, None))
    return jax.shard_map(shards, mesh=mesh, in_specs=in_specs, out_specs=out_specs, check_vma=False)
```

```python
import functools
import math

import jax
import jax.numpy as jnp
from jax import lax
from jax.experimental import pallas as pl
from jax.experimental.pallas import tpu as pltpu
from jax.sharding import PartitionSpec as P

MESH = pl.DeviceIdType.MESH
F32 = jnp.float32
BF16 = jnp.bfloat16

K = 48
C = 3
CX = 2
GY = 16
GZ = 128
CELLS = CX * GY * GZ
ROWS = C * CELLS
NSUB = 8
NROW = 64
PLANES = NROW * CX
SLAB = 4096
CHUNK = 512
NCHUNK = SLAB // CHUNK
BACK = 3
UP = [(1, n) for n in range(NCHUNK - BACK)] + [(0, n) for n in range(NCHUNK)]
DOWN = [(1, n) for n in range(NCHUNK - BACK, NCHUNK)]
BEFORE = 3
PIECE = 16
FAR_FIRST = (4, 3, 5, 2, 6, 1, 7)
NLEVEL = 16
GROUP = 8
OWNERS = 6
LANES = 128
HALF = 64
STRIPS = 8
STEP = 8
STRIP = SLAB // STRIPS
PARTS = 2


def at_sub(sub, by):
    return lax.rem(sub + (by + NSUB), NSUB)


def start_barrier(sub, row):
    z, place = row // GROUP, lax.rem(row, GROUP)
    barrier = pltpu.get_barrier_semaphore()

    def signal(to_sub, to_row):
        pl.semaphore_signal(barrier, inc=1, device_id=(to_sub, to_row), device_id_type=MESH)

    @pl.when(row > 0)
    def _():
        signal(sub, row - 1)

    @pl.when(row < NROW - 1)
    def _():
        signal(sub, row + 1)

    for by in (-1, -2, 2):
        signal(at_sub(sub, by), row)
    for step in FAR_FIRST:
        signal(sub, z * GROUP + lax.rem(place + step, GROUP))

    @pl.when(place < OWNERS)
    def _():
        for step in FAR_FIRST:
            signal(sub, lax.rem(z + step, 8) * GROUP + place)

    for by in (2, -2, 1):
        for q in range(OWNERS):
            signal(at_sub(sub, by), z * GROUP + q)

    owner = (place < OWNERS).astype(jnp.int32)
    sides = (row > 0).astype(jnp.int32) + (row < NROW - 1).astype(jnp.int32)
    return barrier, sides + 3 + (GROUP - 1) + owner * (7 + 3 * GROUP)


def gather(index, table, dest, first):
    def body(step, carry):
        for part in range(PARTS):
            start = pl.multiple_of((step * PARTS + part) * (STRIPS * STEP), STRIPS * STEP)
            at = first // STRIPS + (step * PARTS + part) * STEP
            for q in range(STRIPS):
                for j in range(STEP):
                    dest[pl.ds(start + (q * STEP + j), 1), :] = table[pl.ds(index[q][at + j], 1), :]
        return carry

    lax.fori_loop(0, CHUNK // (PARTS * STRIPS * STEP), body, 0)


def widen(tile):
    return jnp.concatenate([tile, jnp.zeros((GZ, LANES - K), F32)], axis=1)


def kernel(
    counts_in, couple_in, stiffness_in, eigen, material, own_rows, send_rows,
    whole_out, forward_out,
    counts, couple, stiffness, eig, halo, mat, coef, field, image, table, image_rows, own_sel, own_kept, send_sel, packed, arrived, down_packed, down_arrived,
    part, sums, zsums, piece, whole, forward,
    load_sem, halo_send, halo_recv, slab_send, slab_recv, down_send, down_recv,
    one_send, one_recv, two_send, two_recv, three_send, three_recv, fwd_send, fwd_recv, index_sem, eigen_sem, *strips,
):
    sub, row = lax.axis_index("sub"), lax.axis_index("row")
    z, place = row // GROUP, lax.rem(row, GROUP)
    loads = [None]
    own_index = [strips[o * STRIPS : (o + 1) * STRIPS] for o in (0, 1)]
    send_index = [strips[(2 + o) * STRIPS : (3 + o) * STRIPS] for o in (0, 1)]
    index_loads = []
    for kind, (rows, index) in enumerate(((own_rows, own_index), (send_rows, send_index))):
        index_loads.append([])
        for o in (1, 0):
            for q in range(STRIPS):
                index_loads[kind].append(pltpu.make_async_copy(
                    rows.at[0, o, pl.ds(q * STRIP, STRIP)], index[o][q], index_sem.at[kind, o, q]))
    for p in range(CX + 2):
        plane = jnp.clip(row * CX + (p - 1), 0, PLANES - 1)
        loads.append(pltpu.make_async_copy(material.at[0, plane], mat.at[p], load_sem.at[1 + p]))
    loads.append(pltpu.make_async_copy(counts_in, counts, load_sem.at[3 + CX]))
    loads.append(pltpu.make_async_copy(couple_in, couple, load_sem.at[4 + CX]))
    loads.append(pltpu.make_async_copy(stiffness_in, stiffness, load_sem.at[5 + CX]))
    def eigen_load(c, p):
        return pltpu.make_async_copy(eigen.at[0, :, c, p], eig.at[:, c, p], eigen_sem.at[c * CX + p])

    loads[3 + CX].start()
    for c in range(C):
        for p in range(CX):
            eigen_load(c, p).start()
    barrier, greetings = start_barrier(sub, row)
    for load in index_loads[0] + loads[1 : 3 + CX] + loads[4 + CX :] + index_loads[1]:
        load.start()
    loads[3 + CX].wait()
    count = counts[0]

    def kept(k):
        return (k < count).astype(F32)

    @pl.when(row == 0)
    def _():
        halo[0] = jnp.zeros((K, C, GY, GZ), BF16)

    @pl.when(row == NROW - 1)
    def _():
        halo[1] = jnp.zeros((K, C, GY, GZ), BF16)

    def across(source, at):
        return source[pl.ds(at, K, stride=C * CX * GY), :]

    def fill_table(block, carry):
        c, p = block // CX, lax.rem(block, CX)
        eigen_load(c, p).wait()
        for k in range(K):
            base = pl.multiple_of(k * (C * CX * GY) + block * GY, GY)
            field[pl.ds(base, GY), :] = eig[k, c, p].astype(F32) * keeps[k]
        for y in range(GY):
            at = block * GY + y
            table[pl.ds(pl.multiple_of(at * GZ, GZ), GZ), :] = widen(across(field, at).T)
        return carry

    keeps = [kept(k) for k in range(K)]
    lax.fori_loop(0, BEFORE, fill_table, 0)

    pl.semaphore_wait(barrier, greetings)
    def piece_of(h, side, to):
        some = pl.ds(h * PIECE, PIECE)
        return pltpu.make_async_remote_copy(
            src_ref=eigen.at[0, some, :, (CX - 1) * (1 - side)], dst_ref=halo.at[side, some],
            send_sem=halo_send.at[side, h], recv_sem=halo_recv.at[side, h],
            device_id=(sub, to), device_id_type=MESH)

    pieces = range(K // PIECE)
    ups = [piece_of(h, 0, jnp.minimum(row + 1, NROW - 1)) for h in pieces]
    downs_x = [piece_of(h, 1, jnp.maximum(row - 1, 0)) for h in pieces]
    for h in pieces:
        @pl.when(row < NROW - 1)
        def _(h=h):
            ups[h].start()

        @pl.when(row > 0)
        def _(h=h):
            downs_x[h].start()

    lax.fori_loop(BEFORE, C * CX, fill_table, 0)

    for load in index_loads[0]:
        load.wait()
    loads[4 + CX].wait()
    lane = lax.broadcasted_iota(jnp.int32, (K, LANES), 1)
    line = lax.broadcasted_iota(jnp.int32, (K, LANES), 0)
    turn = [
        jnp.where(lane == line, couple[0, o].astype(F32), F32(0)).astype(BF16) for o in (0, 1)]
    plain = jnp.where(lane == line, F32(1), F32(0)).astype(BF16)

    def turned(by, rows):
        return jnp.concatenate([
            lax.dot_general(by, rows[base : base + 256].astype(BF16), (((1,), (1,)), ((), ())),
                            preferred_element_type=F32).astype(BF16)
            for base in range(0, CHUNK, 256)], axis=1)

    slabs = []
    for e, (o, n) in enumerate(UP):
        gather(own_index[o], table, own_sel.at[e % 2], n * CHUNK)
        packed[e] = turned(turn[o], own_sel[e % 2])
        slab = pltpu.make_async_remote_copy(
            src_ref=packed.at[e], dst_ref=arrived.at[e],
            send_sem=slab_send.at[e], recv_sem=slab_recv.at[e],
            device_id=(at_sub(sub, o + 1), row), device_id_type=MESH)
        slab.start()
        slabs.append(slab)
    for p in range(CX + 2):
        loads[1 + p].wait()
    loads[5 + CX].wait()
    kappa = []
    for p in range(CX + 2):
        level = mat[p]
        found = jnp.zeros((GY, GZ), F32)
        for m in range(NLEVEL):
            found = found + jnp.where(level == m, stiffness[m], F32(0))
        kappa.append(found)
    faces = []
    for p in range(CX + 1):
        face = 0.5 * (kappa[p] + kappa[p + 1])
        if p == 0:
            face = face * (row > 0).astype(F32)
        if p == CX:
            face = face * (row < NROW - 1).astype(F32)
        coef[p] = face
        faces.append(face)
    in_y = lax.broadcasted_iota(jnp.int32, (GY, GZ), 0) < GY - 1
    in_z = lax.broadcasted_iota(jnp.int32, (GY, GZ), 1) < GZ - 1
    for p in range(CX):
        mid = kappa[p + 1]
        y_up = jnp.where(in_y, 0.5 * (mid + pltpu.roll(mid, GY - 1, 0)), 0.0)
        z_up = jnp.where(in_z, 0.5 * (mid + pltpu.roll(mid, GZ - 1, 1)), 0.0)
        y_down, z_down = pltpu.roll(y_up, 1, 0), pltpu.roll(z_up, 1, 1)
        for n, face in enumerate((y_down, y_up, z_down, z_up)):
            coef[CX + 1 + 4 * p + n] = face
        along = (faces[p] + faces[p + 1], y_down + y_up, z_down + z_up)
        for c in range(C):
            coef[5 * CX + 1 + C * p + c] = along[0] + along[1] + along[2] + 2.0 * along[c]

    def apply_column(k):
        keep = kept(k)
        for c in range(C):
            def at(p):
                return pl.multiple_of(k * (C * CX * GY) + (c * CX + p) * GY, GY)

            cells = [halo[0, k, c].astype(F32) * keep]
            cells += [field[pl.ds(at(p), GY), :] for p in range(CX)]
            cells.append(halo[1, k, c].astype(F32) * keep)
            for p in range(CX):
                u = cells[p + 1]
                face = [coef[CX + 1 + 4 * p + n] for n in range(4)]
                near = [
                    coef[p] * cells[p] + coef[p + 1] * cells[p + 2],
                    face[0] * pltpu.roll(u, 1, 0) + face[1] * pltpu.roll(u, GY - 1, 0),
                    face[2] * pltpu.roll(u, 1, 1) + face[3] * pltpu.roll(u, GZ - 1, 1),
                ]
                own = coef[5 * CX + 1 + C * p + c]
                image[pl.ds(at(p), GY), :] = own * u - (near[0] + near[1] + near[2] + 2.0 * near[c])

    def apply_columns(block, carry):
        for u in range(4):
            apply_column(4 * block + u)
        return carry

    for h in pieces:
        @pl.when(row > 0)
        def _(h=h):
            ups[h].wait_recv()

        @pl.when(row < NROW - 1)
        def _(h=h):
            downs_x[h].wait_recv()

        lax.fori_loop(h * PIECE // 4, (h + 1) * PIECE // 4, apply_columns, 0)

    def image_table(block, total):
        basis, turned = [], []
        for y in range(GY):
            at = block * GY + y
            wide = widen(across(image, at).T)
            image_rows[pl.ds(pl.multiple_of(at * GZ, GZ), GZ), :] = wide
            turned.append(wide.astype(BF16))
            basis.append(across(field, at).astype(BF16))
        return total + jnp.dot(
            jnp.concatenate(basis, axis=1), jnp.concatenate(turned, axis=0), preferred_element_type=F32)

    diag = lax.fori_loop(0, C * CX, image_table, jnp.zeros((K, LANES), F32))

    for load in index_loads[1]:
        load.wait()
    downs = []
    for e, (o, n) in enumerate(DOWN):
        gather(send_index[o], image_rows, own_sel.at[e % 2], n * CHUNK)
        down_packed[e] = turned(plain, own_sel[e % 2])
        slab = pltpu.make_async_remote_copy(
            src_ref=down_packed.at[e], dst_ref=down_arrived.at[e],
            send_sem=down_send.at[e], recv_sem=down_recv.at[e],
            device_id=(at_sub(sub, -o - 1), row), device_id_type=MESH)
        slab.start()
        downs.append(slab)
    for e, (o, n) in enumerate(DOWN):
        gather(own_index[o], table, own_kept.at[e], n * CHUNK)

    pairs = [jnp.zeros((K, LANES), F32) for o in (0, 1)]
    for e, (o, n) in enumerate(UP):
        gather(send_index[o], image_rows, send_sel.at[e % 2], n * CHUNK)
        slabs[e].wait_recv()
        pairs[o] = pairs[o] + jnp.dot(
            arrived[e], send_sel[e % 2].astype(BF16), preferred_element_type=F32)
    below = jnp.zeros((K, LANES), F32)
    for e in range(BACK):
        downs[e].wait_recv()
        below = below + jnp.dot(
            down_arrived[e], own_kept[e].astype(BF16), preferred_element_type=F32)
    below = below * couple[0, 1].astype(F32)
    mats = [diag + pltpu.roll(pairs[0], HALF, 1), pairs[1] + pltpu.roll(below, HALF, 1)]
    for q in range(OWNERS):
        for m in range(2):
            part[q, pl.ds(8 * m, 8), :] = mats[m][8 * q : 8 * q + 8]

    is_owner = place < OWNERS
    own_q = jnp.minimum(place, OWNERS - 1)

    def landed(ref, sem):
        pltpu.make_async_copy(ref, ref, sem).wait()

    firsts = []
    for step in FAR_FIRST:
        to = lax.rem(place + step, GROUP)
        to_q = jnp.minimum(to, OWNERS - 1)
        firsts.append((to, pltpu.make_async_remote_copy(
            src_ref=part.at[to_q], dst_ref=sums.at[place],
            send_sem=one_send.at[step], recv_sem=one_recv,
            device_id=(sub, z * GROUP + to), device_id_type=MESH)))
    for to, copy in firsts:
        @pl.when(to < OWNERS)
        def _(copy=copy):
            copy.start()

    seconds = []
    for step in FAR_FIRST:
        seconds.append(pltpu.make_async_remote_copy(
            src_ref=piece.at[0], dst_ref=zsums.at[z],
            send_sem=two_send, recv_sem=two_recv,
            device_id=(sub, lax.rem(z + step, 8) * GROUP + place), device_id_type=MESH))

    thirds = []
    for o, by in ((1, -2), (2, 2), (0, -1)):
        for to in range(GROUP):
            thirds.append(pltpu.make_async_remote_copy(
                src_ref=piece.at[1, pl.ds(8 if o else 0, 8)], dst_ref=forward.at[o, own_q],
                send_sem=fwd_send.at[o], recv_sem=fwd_recv,
                device_id=(at_sub(sub, by), z * GROUP + to), device_id_type=MESH))
    for step in FAR_FIRST:
        thirds.append(pltpu.make_async_remote_copy(
            src_ref=piece.at[1], dst_ref=whole.at[own_q],
            send_sem=three_send, recv_sem=three_recv,
            device_id=(sub, z * GROUP + lax.rem(place + step, GROUP)), device_id_type=MESH))

    for h in pieces:
        @pl.when(row < NROW - 1)
        def _(h=h):
            ups[h].wait_send()

        @pl.when(row > 0)
        def _(h=h):
            downs_x[h].wait_send()

    for slab in slabs + downs:
        slab.wait_send()

    @pl.when(is_owner)
    def _():
        sums[place] = part[own_q]
        landed(sums.at[pl.ds(0, GROUP - 1)], one_recv)
        total = sums[0]
        for q in range(1, GROUP):
            total = total + sums[q]
        piece[0] = total
        for copy in seconds:
            copy.start()
        zsums[z] = total
        landed(zsums.at[pl.ds(0, 7)], two_recv)
        total = zsums[0]
        for q in range(1, 8):
            total = total + zsums[q]
        piece[1] = total
        for copy in thirds:
            copy.start()
        whole[own_q] = total
        landed(zsums.at[pl.ds(0, 7)], two_send)
        landed(whole.at[pl.ds(0, OWNERS - 1)], three_recv)

    for to, copy in firsts:
        @pl.when(to < OWNERS)
        def _(copy=copy):
            copy.wait_send()

    @pl.when(place >= OWNERS)
    def _():
        landed(whole, three_recv)

    landed(forward, fwd_recv)

    whole_out[...] = whole[...]
    forward_out[...] = forward[...]

    @pl.when(is_owner)
    def _():
        for o in range(3):
            landed(sums.at[pl.ds(0, GROUP // 2)], fwd_send.at[o])
        landed(sums.at[pl.ds(0, GROUP - 1)], three_send)


def assemble(whole, forward, diag_out, off_out):
    scale = 1.0 / math.sqrt(NROW * SLAB)
    diag_pair, pair_below = [
        jnp.concatenate([whole[q, at : at + 8] for q in range(OWNERS)], axis=0) for at in (0, 8)]
    from_above = [jnp.concatenate([forward[o, q] for q in range(OWNERS)], axis=0) for o in range(3)]
    diag_out[0] = diag_pair[:, :K] * (1.0 / (C * PLANES * GY * GZ))
    off_out[0, 0] = (pair_below.T[:K] + pltpu.roll(from_above[2], HALF, 1)[:, :K]) * scale
    off_out[0, 1] = diag_pair.T[HALF : HALF + K] * scale
    off_out[0, 2] = pltpu.roll(from_above[0], HALF, 1)[:, :K] * scale
    off_out[0, 3] = (from_above[1][:, :K] + pair_below.T[HALF : HALF + K]) * scale


def shards(eigen_basis, material, counts, couple, own_rows, send_rows, stiffness):
    hbm = pl.BlockSpec(memory_space=pltpu.HBM)
    vmem = pl.BlockSpec(memory_space=pltpu.VMEM)
    dma = pltpu.SemaphoreType.DMA
    sums = pl.pallas_call(
        kernel,
        out_shape=(
            jax.ShapeDtypeStruct((OWNERS, 16, LANES), F32),
            jax.ShapeDtypeStruct((3, OWNERS, 8, LANES), F32),
        ),
        in_specs=[hbm] * 7,
        out_specs=(vmem, vmem),
        scratch_shapes=[
            pltpu.SMEM((1,), jnp.int32),
            pltpu.SMEM((1, 2), jnp.int32),
            pltpu.SMEM((NLEVEL,), F32),
            pltpu.VMEM((K, C, CX, GY, GZ), BF16),
            pltpu.VMEM((2, K, C, GY, GZ), BF16),
            pltpu.VMEM((CX + 2, GY, GZ), jnp.int32),
            pltpu.VMEM((5 * CX + 1 + C * CX, GY, GZ), F32),
            pltpu.VMEM(((K + 1) * C * CX * GY, GZ), F32),
            pltpu.VMEM(((K + 1) * C * CX * GY, GZ), F32),
            pltpu.VMEM((ROWS, LANES), F32),
            pltpu.VMEM((ROWS, LANES), F32),
            pltpu.VMEM((2, CHUNK, LANES), F32),
            pltpu.VMEM((BACK, CHUNK, LANES), F32),
            pltpu.VMEM((2, CHUNK, LANES), F32),
            pltpu.VMEM((len(UP), K, CHUNK), BF16),
            pltpu.VMEM((len(UP), K, CHUNK), BF16),
            pltpu.VMEM((BACK, K, CHUNK), BF16),
            pltpu.VMEM((BACK, K, CHUNK), BF16),
            pltpu.VMEM((OWNERS, 16, LANES), F32),
            pltpu.VMEM((GROUP, 16, LANES), F32),
            pltpu.VMEM((8, 16, LANES), F32),
            pltpu.VMEM((2, 16, LANES), F32),
            pltpu.VMEM((OWNERS, 16, LANES), F32),
            pltpu.VMEM((3, OWNERS, 8, LANES), F32),
            dma((6 + CX,)), dma((2, K // PIECE)), dma((2, K // PIECE)), dma((len(UP),)), dma((len(UP),)), dma((BACK,)), dma((BACK,)),
            dma((GROUP,)), dma, dma, dma, dma, dma, dma((3,)), dma,
            dma((2, 2, STRIPS)), dma((C * CX,)),
        ] + [pltpu.SMEM((STRIP,), jnp.int32) for _ in range(4 * STRIPS)],
        compiler_params=pltpu.CompilerParams(
            collective_id=0, has_side_effects=True, vmem_limit_bytes=60 * 2**20),
        name="coarse",
    )(counts, couple, stiffness, eigen_basis, material, own_rows, send_rows)
    return pl.pallas_call(
        assemble,
        out_shape=(jax.ShapeDtypeStruct((1, K, K), F32), jax.ShapeDtypeStruct((1, 4, K, K), F32)),
        in_specs=[vmem, vmem],
        out_specs=(vmem, vmem),
        name="assemble",
    )(*sums)


def solution(mesh):
    in_specs = (
        P("sub", None, None, "row", None, None),
        P("sub", None, None, None),
        P("sub"),
        P("sub", None),
        P("sub", None, "row"),
        P("sub", None, "row"),
        P(),
    )
    out_specs = (P("sub", None, None), P("sub", None, None, None))
    return jax.shard_map(shards, mesh=mesh, in_specs=in_specs, out_specs=out_specs, check_vma=False)
```
